256 devices in a mesh: gx: 16 (over z, core), gy: 16 (over x, y).
Axes of the slice: x: 4, y: 4, z: 8, core: 2. Of those that a mesh axis runs over, the one named last changes fastest.
Arguments:
- state: float32 [5, 1, 4096, 4096], P(None, None, 'gx', 'gy'), may hold values from -1.6 to 6.4, as said below
- viscous: float32 [1, 4096, 4096], P(None, 'gx', 'gy'), may hold values from 0.5 to 2000000
Outputs:
- new_state: float32 [5, 1, 4096, 4096], P(None, None, 'gx', 'gy')
The draws below stay inside these ranges and needn't reach their ends.
Inputs may be any that keep to these rules, and one draw needn't show every extreme that they name: state[0] and 0.4 (state[4] - 0.5 (state[1]^2 + state[2]^2 + state[3]^2) / state[0]) lie between 0.6 and 1.6 in every cell.
All inputs are finite; a program needn't handle non-finite values.
Results may differ from the reference program's by a relative error of at most 0.00055.
Values sent between devices are 32-bit elements; how exact they have to be, the bound alone decides.
No kernel may reach another device: no remote copies, remote signals or barrier semaphores. Data moves between devices by JAX's collectives and lax.ppermute only.
A program may use at most 128 MiB of HBM per device.

```python
import math
import jax
import jax.numpy as jnp
from jax import lax

NX = 4096
NY = 4096
NZ = 1


def draw_state(key, part):
    key = jax.random.fold_in(key, 11)
    density_key, pressure_key, velocity_key = jax.random.split(key, 3)
    grid_shape = (NZ, NX, NY)
    density = jax.random.uniform(density_key, grid_shape, jnp.float32, 0.6, 1.6)
    pressure_cell = jax.random.uniform(pressure_key, grid_shape, jnp.float32, 0.6, 1.6)
    velocity = jnp.clip(0.35 * jax.random.normal(velocity_key, (3,) + grid_shape, jnp.float32), -1.0, 1.0)
    momentum = density * velocity
    speed_sq = velocity[0] * velocity[0] + velocity[1] * velocity[1] + velocity[2] * velocity[2]
    energy = pressure_cell / 0.4 + 0.5 * density * speed_sq
    return jnp.concatenate([density[None], momentum, energy[None]], 0)


def draw_viscous(key, part):
    key = jax.random.fold_in(key, 23)
    order_key, jitter_key, cell_key = jax.random.split(key, 3)
    high_log = math.log(1000000.0)
    ranking = jax.random.permutation(order_key, NZ).astype(jnp.float32)
    jitter = jax.random.uniform(jitter_key, (NZ,), jnp.float32, 0.5, 1.0)
    position = jnp.where(ranking < 0.5, 0.0, (ranking + jitter) / NZ)
    plane_scale = jnp.exp(high_log * position)
    cell_factor = jax.random.uniform(cell_key, (NZ, NX, NY), jnp.float32, 0.5, 2.0)
    return cell_factor * plane_scale[:, None, None]


def setup_inputs(seed: int = 0) -> dict:
    key_of = jax.random.split(jax.random.key(seed), 3)
    state = draw_state(jax.random.fold_in(key_of[2], 71), 0)
    viscous = draw_viscous(jax.random.fold_in(key_of[2], 71), 0)
    return {"state": state, "viscous": viscous}


STEP_RATIO = 0.25
ONE_THIRD = 1.0 / 3.0
NEAR_WEIGHT = 7.0 / 9.0
FAR_WEIGHT = 1.0 / 36.0
GAMMA_MINUS = 0.4

def pressure(fields, density):
    kinetic = fields[1] * fields[1] + fields[2] * fields[2] + fields[3] * fields[3]
    return GAMMA_MINUS * (fields[4] - 0.5 * kinetic / density)

def shifter(values, along_dim):
    extent = values.shape[along_dim]
    widths = [(0, 0)] * values.ndim
    widths[along_dim] = (2, 2)
    padded = jnp.pad(values, widths)

    def shifted_by(offset):
        return lax.slice_in_dim(padded, 2 + offset, 2 + offset + extent, axis=along_dim)
    return shifted_by

def mass_term(values, along_dim):
    shifted_by = shifter(values, along_dim)
    return shifted_by(0) + ONE_THIRD * (shifted_by(-1) + shifted_by(1))

def central_term(values, along_dim):
    shifted_by = shifter(values, along_dim)
    return NEAR_WEIGHT * (shifted_by(1) - shifted_by(-1)) + FAR_WEIGHT * (shifted_by(2) - shifted_by(-2))

def line_matrix(viscous, along_dim):
    shifted_by = shifter(viscous, along_dim)
    middle = shifted_by(0)
    face_low = 0.5 * (shifted_by(-1) + middle)
    face_high = 0.5 * (middle + shifted_by(1))
    return (ONE_THIRD - face_low, 1.0 + face_low + face_high, ONE_THIRD - face_high)

def solve_lines(lower, diagonal, upper, source, along_dim):
    extent = diagonal.shape[along_dim]
    row_ids = lax.broadcasted_iota(jnp.int32, diagonal.shape, along_dim)
    lower = jnp.where(row_ids == 0, jnp.zeros_like(lower), lower)
    upper = jnp.where(row_ids == extent - 1, jnp.zeros_like(upper), upper)
    solved = lax.linalg.tridiagonal_solve(jnp.moveaxis(lower, along_dim, -1), jnp.moveaxis(diagonal, along_dim, -1), jnp.moveaxis(upper, along_dim, -1), jnp.moveaxis(source, (0, along_dim + 1), (-1, -2)))
    return jnp.moveaxis(solved, (-1, -2), (0, along_dim + 1))

def plane_step(plane_pair):
    plane_state, plane_viscous = plane_pair
    density = plane_state[0]
    velocity_x = plane_state[1] / density
    velocity_y = plane_state[2] / density
    pressure_cell = pressure(plane_state, density)
    flux_x = jnp.stack([plane_state[1], plane_state[1] * velocity_x + pressure_cell, plane_state[2] * velocity_x, plane_state[3] * velocity_x, (plane_state[4] + pressure_cell) * velocity_x])
    source_x = mass_term(plane_state, 1) - STEP_RATIO * central_term(flux_x, 1)
    lower, diagonal, upper = line_matrix(plane_viscous, 0)
    x_section = solve_lines(lower, diagonal, upper, source_x, 0)
    flux_y = jnp.stack([velocity_y * x_section[0], velocity_y * x_section[1], velocity_y * x_section[2] + pressure_cell, velocity_y * x_section[3], velocity_y * x_section[4] + pressure_cell * velocity_y])
    source_y = mass_term(x_section, 2) - STEP_RATIO * central_term(flux_y, 2)
    lower, diagonal, upper = line_matrix(plane_viscous, 1)
    return solve_lines(lower, diagonal, upper, source_y, 1)

def reference(state, viscous):
    planes = lax.map(plane_step, (jnp.moveaxis(state, 1, 0), viscous))
    return jnp.moveaxis(planes, 0, 1)
```

```python
import functools
import jax
import jax.numpy as jnp
from jax import lax
from jax.experimental import pallas as pl
from jax.experimental.pallas import tpu as pltpu
from jax.sharding import PartitionSpec as P

STEP_RATIO = 0.25
ONE_THIRD = 1.0 / 3.0
NEAR_WEIGHT = 7.0 / 9.0
FAR_WEIGHT = 1.0 / 36.0
GAMMA_MINUS = 0.4
FAR_SCALED = STEP_RATIO * FAR_WEIGHT
FIELDS = 5
CHUNKS = 8
LANES = 128
PAY_ROWS = 40
ROW_RIGHT, ROW_HI, ROW_FLUX_RIGHT, ROW_LEFT, ROW_FLUX_LEFT, ROW_LO = 16, 21, 22, 27, 32, 37


def strided(ref, position, count):
    return ref[pl.ds(position, CHUNKS, stride=count), :]


def sublane_ids(shape):
    return lax.broadcasted_iota(jnp.int32, shape, 0)


def from_previous(value):
    return jnp.where(sublane_ids(value.shape) == 0, 0.0, pltpu.roll(value, 1, 0))


def from_next(value):
    return jnp.where(sublane_ids(value.shape) == CHUNKS - 1, 0.0, pltpu.roll(value, CHUNKS - 1, 0))


class Window:
    def __init__(self, make, count):
        self.make, self.count, self.known = make, count, {}

    def __call__(self, position):
        if position not in self.known:
            if position < 0:
                value = jax.tree.map(from_previous, self(position + self.count))
            elif position >= self.count:
                value = jax.tree.map(from_next, self(position - self.count))
            else:
                value = self.make(position)
            self.known[position] = value
        return self.known[position]


def local_solve(cells, viscous, count, part_ref, left_ref, right_ref, inner_ref, pay_ref, first_ref, last_ref):
    final = count - 1

    @functools.cache
    def face(j):
        return 0.5 * (viscous(j - 1) + viscous(j))

    @functools.cache
    def coupling(j):
        return ONE_THIRD - face(j)

    def diagonal(j):
        return 1.0 + face(j) + face(j + 1)

    def source(j, q):
        u_low, u_mid, u_high = cells(j - 1)[0][q], cells(j)[0][q], cells(j + 1)[0][q]
        f = [cells(j + o)[1][q] for o in (-2, -1, 1, 2)]
        central = NEAR_WEIGHT * (f[2] - f[1]) + FAR_WEIGHT * (f[3] - f[0])
        return u_mid + ONE_THIRD * (u_low + u_high) - STEP_RATIO * central

    rows = lambda j: pl.ds(j * CHUNKS, CHUNKS)
    slopes = {}
    forward = left = None
    ends = {}
    for j in range(count):
        values = [source(j, q) for q in range(FIELDS)]
        if j == 0 or j == final:
            ends[j] = values
            continue
        if j == 1:
            inverse = 1.0 / diagonal(j)
            left = -coupling(j) * inverse
            forward = [s * inverse for s in values]
        else:
            inverse = 1.0 / (diagonal(j) - coupling(j) * slopes[j - 1])
            tied = coupling(j) * inverse
            left = -tied * left
            forward = [s * inverse - tied * f for s, f in zip(values, forward)]
        slopes[j] = coupling(j + 1) * inverse
        left_ref[rows(j), :] = left
        right_ref[rows(j), :] = slopes[j]
        for q in range(FIELDS):
            part_ref[q, rows(j), :] = forward[q]
    last_part, last_left, last_right = forward, left, -slopes[final - 1]
    right = last_right
    right_ref[rows(final - 1), :] = right
    for j in range(final - 2, 0, -1):
        slope = right_ref[rows(j), :]
        left = left_ref[rows(j), :] - slope * left
        right = -slope * right
        forward = [part_ref[q, rows(j), :] - slope * f for q, f in enumerate(forward)]
        left_ref[rows(j), :] = left
        right_ref[rows(j), :] = right
        for q in range(FIELDS):
            part_ref[q, rows(j), :] = forward[q]
    zeros = jnp.zeros_like(left)
    up_first, low_last = coupling(1), coupling(final)
    first_diag = diagonal(0) + up_first * left
    first_up = up_first * right
    last_low = low_last * last_left
    last_diag = diagonal(final) + low_last * last_right
    first_low, last_up = coupling(0), coupling(count)
    for q in range(FIELDS):
        first_ref[pl.ds(q, CHUNKS, stride=8), :] = ends[0][q] - up_first * forward[q]
        last_ref[pl.ds(q, CHUNKS, stride=8), :] = ends[final][q] - low_last * last_part[q]
    ids = sublane_ids(zeros.shape)
    first_ref[pl.ds(5, CHUNKS, stride=8), :] = zeros
    first_ref[pl.ds(6, CHUNKS, stride=8), :] = jnp.where(ids == CHUNKS - 1, -first_up, zeros)
    first_ref[pl.ds(7, CHUNKS, stride=8), :] = zeros
    last_ref[pl.ds(5, CHUNKS, stride=8), :] = jnp.where(ids == 0, -last_low, zeros)
    last_ref[pl.ds(6, CHUNKS, stride=8), :] = zeros
    last_ref[pl.ds(7, CHUNKS, stride=8), :] = zeros

    def row(value, c):
        return value[c : c + 1]

    block = lambda ref, c: ref[pl.ds(8 * c, 8), :]
    chain = []
    for c in range(CHUNKS):
        if c > 0:
            chain.append((row(first_low, c), row(first_diag, c), row(first_up, c), block(first_ref, c)))
        if c < CHUNKS - 1:
            chain.append((row(last_low, c), row(last_diag, c), row(last_up, c), block(last_ref, c)))
    solved, chain_slopes = [], []
    for m, (low, diag, up, rhs) in enumerate(chain):
        if m == 0:
            inverse = 1.0 / diag
            solved.append(rhs * inverse)
        else:
            inverse = 1.0 / (diag - low * chain_slopes[-1])
            solved.append((rhs - low * solved[-1]) * inverse)
        chain_slopes.append(up * inverse)
    for m in range(len(chain) - 2, -1, -1):
        solved[m] = solved[m] - chain_slopes[m] * solved[m + 1]
    inner_ref[0:8, :] = jnp.zeros_like(solved[0])
    inner_ref[120:128, :] = jnp.zeros_like(solved[0])
    for m, value in enumerate(solved):
        inner_ref[8 * m + 8 : 8 * m + 16, :] = value

    for q in range(FIELDS):
        pay_ref[q : q + 1, :] = row(forward[q], 0)
        pay_ref[8 + q : 9 + q, :] = row(last_part[q], CHUNKS - 1)
    pay_ref[5:6, :] = row(left, 0)
    pay_ref[6:8, :] = jnp.zeros((2, zeros.shape[1]), jnp.float32)
    pay_ref[13:14, :] = jnp.zeros((1, zeros.shape[1]), jnp.float32)
    pay_ref[14:15, :] = row(last_right, CHUNKS - 1)
    pay_ref[15:16, :] = jnp.zeros((1, zeros.shape[1]), jnp.float32)
    eight = sublane_ids((8, zeros.shape[1]))
    second = pay_ref[0:8, :] + row(right, 0) * solved[0]
    pay_ref[0:8, :] = jnp.where(eight < FIELDS, -row(up_first, 0) * second, second)
    before = pay_ref[8:16, :] + row(last_left, CHUNKS - 1) * solved[-1]
    pay_ref[8:16, :] = jnp.where(eight < FIELDS, -row(low_last, CHUNKS - 1) * before, before)
    for q in range(FIELDS):
        pay_ref[q : q + 1, :] += row(ends[0][q], 0)
        pay_ref[8 + q : 9 + q, :] += row(ends[final][q], CHUNKS - 1)
    write_payload(cells, viscous, face, count, pay_ref)


def write_payload(cells, viscous, face, count, pay_ref):
    final = count - 1
    first = lambda value: value[0:1]
    last = lambda value: value[CHUNKS - 1 : CHUNKS]
    pay_ref[7:8, :] = first(viscous(0))
    pay_ref[15:16, :] = last(viscous(final))
    pay_ref[ROW_HI : ROW_HI + 1, :] = first(face(1))
    pay_ref[ROW_LO : ROW_LO + 1, :] = last(face(final))
    u_last, f_last = cells(final)
    f_before = cells(final - 1)[1]
    u_first, f_first = cells(0)
    f_second = cells(1)[1]
    for q in range(FIELDS):
        right = ONE_THIRD * last(u_last[q]) + STEP_RATIO * (
            NEAR_WEIGHT * last(f_last[q]) + FAR_WEIGHT * last(f_before[q])
        )
        left = ONE_THIRD * first(u_first[q]) - STEP_RATIO * (
            NEAR_WEIGHT * first(f_first[q]) + FAR_WEIGHT * first(f_second[q])
        )
        pay_ref[ROW_RIGHT + q : ROW_RIGHT + q + 1, :] = right
        pay_ref[ROW_FLUX_RIGHT + q : ROW_FLUX_RIGHT + q + 1, :] = last(f_last[q])
        pay_ref[ROW_LEFT + q : ROW_LEFT + q + 1, :] = left
        pay_ref[ROW_FLUX_LEFT + q : ROW_FLUX_LEFT + q + 1, :] = first(f_first[q])
    pay_ref[38:40, :] = jnp.zeros((2, pay_ref.shape[1]), jnp.float32)


def reduced_solve(me, devices, half, all_ref, coef_ref, out_ref):
    def quantity(row):
        return all_ref[pl.ds(half * PAY_ROWS + row, devices, stride=2 * PAY_ROWS), :]

    first_v, last_v = quantity(7), quantity(15)
    hi_first, lo_last = quantity(ROW_HI), quantity(ROW_LO)
    ids = sublane_ids(first_v.shape)
    at_start, at_end = ids == 0, ids == devices - 1
    v_below = jnp.where(at_start, 0.0, pltpu.roll(last_v, 1, 0))
    v_above = jnp.where(at_end, 0.0, pltpu.roll(first_v, devices - 1, 0))
    lo_first = 0.5 * (v_below + first_v)
    hi_last = 0.5 * (last_v + v_above)
    up_first = ONE_THIRD - hi_first
    low_last = ONE_THIRD - lo_last
    table = (
        jnp.where(at_start, 0.0, ONE_THIRD - lo_first),
        (1.0 + lo_first + hi_first) + up_first * quantity(5),
        up_first * quantity(6),
        low_last * quantity(13),
        (1.0 + lo_last + hi_last) + low_last * quantity(14),
        jnp.where(at_end, 0.0, ONE_THIRD - hi_last),
        1.0 / up_first,
        1.0 / low_last,
    )
    for i, value in enumerate(table):
        coef_ref[i * devices : (i + 1) * devices, :] = value

    def coef(i, d):
        return coef_ref[i * devices + d : i * devices + d + 1, :]

    def piece(d, row, size=8):
        return all_ref[pl.ds((2 * d + half) * PAY_ROWS + row, size), :]

    def one(d, row):
        return piece(d, row, 1)

    slope = value = None
    steps, deltas = [], []
    for d in range(devices):
        rhs_first, rhs_last = piece(d, 0), piece(d, 8)
        delta_second = delta_before = None
        if d > 0:
            delta_second = FAR_SCALED * piece(d - 1, ROW_FLUX_RIGHT)
            rhs_first = rhs_first + piece(d - 1, ROW_RIGHT) + one(d, 5) * delta_second
            rhs_last = rhs_last + one(d, 6) * delta_second
        if d < devices - 1:
            delta_before = -FAR_SCALED * piece(d + 1, ROW_FLUX_LEFT)
            rhs_first = rhs_first + one(d, 13) * delta_before
            rhs_last = rhs_last + piece(d + 1, ROW_LEFT) + one(d, 14) * delta_before
        deltas.append((delta_second, delta_before))
        for base, rhs in ((0, rhs_first), (3, rhs_last)):
            if slope is None:
                inverse = 1.0 / coef(base + 1, d)
                value = rhs * inverse
            else:
                inverse = 1.0 / (coef(base + 1, d) - coef(base, d) * slope)
                value = (rhs - coef(base, d) * value) * inverse
            slope = coef(base + 2, d) * inverse
            steps.append((slope, value))
    following = None
    for d in range(devices - 1, -1, -1):
        x_last = steps[2 * d + 1][1]
        if following is not None:
            x_last = x_last - steps[2 * d + 1][0] * following
        x_first = steps[2 * d][1] - steps[2 * d][0] * x_last
        following = x_first
        delta_second, delta_before = deltas[d]
        seen_first = x_first if delta_second is None else x_first - delta_second * coef(6, d)
        seen_last = x_last if delta_before is None else x_last - delta_before * coef(7, d)
        for i, value in enumerate((x_first, x_last, seen_first, seen_last)):
            out_ref[d * 32 + 8 * i : d * 32 + 8 * i + 8, :] = value
    start = pl.multiple_of(me * 32, 32)
    mine = out_ref[pl.ds(start, 32), :]
    return mine[0:8], mine[8:16], mine[16:24], mine[24:32]


def rebuild(ends, count, part_ref, left_ref, right_ref, inner_ref, sol_ref, store):
    x_first, x_last, seen_first, seen_last = ends
    for m in range(16):
        if m == 0:
            value = seen_first
        elif m == 15:
            value = seen_last
        else:
            inner = inner_ref[8 * m : 8 * m + 8, :]
            value = inner + inner[5:6] * seen_first + inner[6:7] * seen_last
        sol_ref[8 * m : 8 * m + 8, :] = value
    chunk_first = [sol_ref[pl.ds(q, CHUNKS, stride=16), :] for q in range(FIELDS)]
    chunk_last = [sol_ref[pl.ds(8 + q, CHUNKS, stride=16), :] for q in range(FIELDS)]
    ids = sublane_ids(chunk_first[0].shape)
    for q in range(FIELDS):
        store(q, 0, jnp.where(ids == 0, x_first[q : q + 1], chunk_first[q]))
        store(q, count - 1, jnp.where(ids == CHUNKS - 1, x_last[q : q + 1], chunk_last[q]))
    for j in range(1, count - 1):
        left, right = left_ref[pl.ds(j * CHUNKS, CHUNKS), :], right_ref[pl.ds(j * CHUNKS, CHUNKS), :]
        for q in range(FIELDS):
            part = part_ref[q, pl.ds(j * CHUNKS, CHUNKS), :]
            store(q, j, part + left * chunk_first[q] + right * chunk_last[q])


def turn(from_ref, to_ref):
    for i in range(2):
        for k in range(2):
            to_ref[k, i * LANES : (i + 1) * LANES, :] = from_ref[i, k * LANES : (k + 1) * LANES, :].T


def x_kernel(
    count, state_ref, viscous_ref, part_ref, left_ref, right_ref, inner_ref, pay_ref, aux_ref, first_ref, last_ref
):
    def make_cells(j):
        density, mom_x, mom_y, mom_z, energy = (strided(state_ref.at[q], j, count) for q in range(FIELDS))
        inverse = 1.0 / density
        vel_x = mom_x * inverse
        kinetic = mom_x * mom_x + mom_y * mom_y + mom_z * mom_z
        press = GAMMA_MINUS * (energy - 0.5 * kinetic * inverse)
        here = pl.ds(j * CHUNKS, CHUNKS)
        aux_ref[0, here, :] = mom_y * inverse
        aux_ref[1, here, :] = press
        flux = (mom_x, mom_x * vel_x + press, mom_y * vel_x, mom_z * vel_x, (energy + press) * vel_x)
        return (density, mom_x, mom_y, mom_z, energy), flux

    def make_viscous(j):
        value = strided(viscous_ref, j, count)
        aux_ref[2, pl.ds(j * CHUNKS, CHUNKS), :] = value
        return value

    local_solve(
        Window(make_cells, count), Window(make_viscous, count), count,
        part_ref, left_ref, right_ref, inner_ref, pay_ref, first_ref, last_ref,
    )


def y_kernel(
    count, devices, me_ref, all_ref, x_part_ref, x_left_ref, x_right_ref, x_inner_ref, aux_ref,
    part_ref, left_ref, right_ref, inner_ref, pay_ref,
    coef_ref, out_ref, sol_ref, section_ref, turned_ref, first_ref, last_ref,
):
    ends = [reduced_solve(me_ref[0], devices, h, all_ref, coef_ref.at[h], out_ref.at[h]) for h in range(2)]
    for h in range(2):
        def store(q, j, value):
            section_ref[q, h, pl.ds(j * CHUNKS, CHUNKS), :] = value

        rebuild(
            ends[h], count, x_part_ref.at[h], x_left_ref.at[h], x_right_ref.at[h], x_inner_ref.at[h],
            sol_ref.at[h], store,
        )
    for q in range(FIELDS):
        turn(section_ref.at[q], turned_ref.at[q])
    for i in range(3):
        turn(aux_ref.at[:, i], turned_ref.at[FIELDS + i])

    def half(h, _):
        def value(q, j):
            return strided(turned_ref.at[q, h], j, count)

        def make_cells(j):
            section = tuple(value(q, j) for q in range(FIELDS))
            vel_y, press = value(FIELDS, j), value(FIELDS + 1, j)
            flux = (
                vel_y * section[0], vel_y * section[1], vel_y * section[2] + press,
                vel_y * section[3], vel_y * section[4] + press * vel_y,
            )
            return section, flux

        local_solve(
            Window(make_cells, count), Window(lambda j: value(FIELDS + 2, j), count), count,
            part_ref.at[h], left_ref.at[h], right_ref.at[h], inner_ref.at[h], pay_ref.at[h], first_ref, last_ref,
        )
        return 0

    lax.fori_loop(0, 2, half, 0)


def last_kernel(
    count, devices, me_ref, all_ref, part_ref, left_ref, right_ref, inner_ref, new_ref,
    coef_ref, out_ref, sol_ref, section_ref, turned_ref,
):
    ends = [reduced_solve(me_ref[0], devices, h, all_ref, coef_ref.at[h], out_ref.at[h]) for h in range(2)]
    for h in range(2):
        def store(q, j, value):
            section_ref[q, h, pl.ds(j, CHUNKS, stride=count), :] = value

        rebuild(
            ends[h], count, part_ref.at[h], left_ref.at[h], right_ref.at[h], inner_ref.at[h], sol_ref.at[h], store
        )
    for q in range(FIELDS):
        turn(section_ref.at[q], turned_ref.at[q])
        for h in range(2):
            for c in range(CHUNKS):
                for k in range(count // 8):
                    rows = turned_ref[q, h, pl.ds(64 * k + c, 8, stride=CHUNKS), :]
                    new_ref[q, c * count + 8 * k : c * count + 8 * k + 8, h * LANES : (h + 1) * LANES] = rows


def shards(devices_x, devices_y, state, viscous):
    cells = state.shape[2]
    count = cells // CHUNKS
    float_of = lambda *shape: jax.ShapeDtypeStruct(shape, jnp.float32)
    memory = lambda *shape: pltpu.VMEM(shape, jnp.float32)
    params = pltpu.CompilerParams(vmem_limit_bytes=48 * 1024 * 1024)
    whole = pl.BlockSpec(memory_space=pltpu.VMEM)
    scalar = pl.BlockSpec(memory_space=pltpu.SMEM)
    solved_shapes = [
        float_of(2, FIELDS, cells, LANES), float_of(2, cells, LANES), float_of(2, cells, LANES),
        float_of(2, 128, LANES), float_of(2, PAY_ROWS, LANES),
    ]
    half_block = lambda *shape: pl.BlockSpec((None,) + shape, lambda h: (h,) + (0,) * len(shape))
    *x_parts, x_pay, aux = pl.pallas_call(
        functools.partial(x_kernel, count),
        grid=(2,),
        out_shape=solved_shapes + [float_of(2, 3, cells, LANES)],
        in_specs=[
            pl.BlockSpec((FIELDS, cells, LANES), lambda h: (0, 0, h)),
            pl.BlockSpec((cells, LANES), lambda h: (0, h)),
        ],
        out_specs=[half_block(*s.shape[1:]) for s in solved_shapes] + [half_block(3, cells, LANES)],
        scratch_shapes=[memory(64, LANES)] * 2,
        compiler_params=params,
        name="x_lines",
    )(state.reshape(FIELDS, cells, cells), viscous.reshape(cells, cells))
    x_all = lax.all_gather(x_pay, "gx").reshape(devices_x * 2 * PAY_ROWS, LANES)
    me_x = lax.axis_index("gx").astype(jnp.int32).reshape(1)
    me_y = lax.axis_index("gy").astype(jnp.int32).reshape(1)
    *y_parts, y_pay = pl.pallas_call(
        functools.partial(y_kernel, count, devices_x),
        out_shape=solved_shapes,
        in_specs=[scalar] + [whole] * 6,
        out_specs=[whole] * 5,
        scratch_shapes=[
            memory(2, 8 * devices_x, LANES), memory(2, 32 * devices_x, LANES), memory(2, 128, LANES),
            memory(FIELDS, 2, cells, LANES), memory(FIELDS + 3, 2, cells, LANES),
            memory(64, LANES), memory(64, LANES),
        ],
        compiler_params=params,
        name="y_lines",
    )(me_x, x_all, *x_parts, aux)
    copies = jnp.broadcast_to(y_pay[None], (devices_y,) + y_pay.shape)
    y_all = lax.all_to_all(copies, "gy", 0, 0).reshape(devices_y * 2 * PAY_ROWS, LANES)
    new = pl.pallas_call(
        functools.partial(last_kernel, count, devices_y),
        out_shape=float_of(FIELDS, cells, cells),
        in_specs=[scalar] + [whole] * 5,
        out_specs=whole,
        scratch_shapes=[
            memory(2, 8 * devices_y, LANES), memory(2, 32 * devices_y, LANES), memory(2, 128, LANES),
            memory(FIELDS, 2, cells, LANES), memory(FIELDS, 2, cells, LANES),
        ],
        compiler_params=params,
        name="new_state",
    )(me_y, y_all, *y_parts)
    return new.reshape(state.shape)


def solution(mesh):
    placed = (P(None, None, "gx", "gy"), P(None, "gx", "gy"))
    return jax.shard_map(
        functools.partial(shards, mesh.shape["gx"], mesh.shape["gy"]),
        mesh=mesh, in_specs=placed, out_specs=P(None, None, "gx", "gy"), check_vma=False,
    )
```

```python
import functools
import jax
import jax.numpy as jnp
from jax import lax
from jax.experimental import pallas as pl
from jax.experimental.pallas import tpu as pltpu
from jax.sharding import PartitionSpec as P

STEP_RATIO = 0.25
ONE_THIRD = 1.0 / 3.0
NEAR_WEIGHT = 7.0 / 9.0
FAR_WEIGHT = 1.0 / 36.0
GAMMA_MINUS = 0.4
FAR_SCALED = STEP_RATIO * FAR_WEIGHT
FIELDS = 5
CHUNKS = 8
LANES = 128
PAY_ROWS = 40
ROW_RIGHT, ROW_HI, ROW_FLUX_RIGHT, ROW_LEFT, ROW_FLUX_LEFT, ROW_LO = 16, 21, 22, 27, 32, 37


def strided(ref, position, count):
    return ref[pl.ds(position, CHUNKS, stride=count), :]


def sublane_ids(shape):
    return lax.broadcasted_iota(jnp.int32, shape, len(shape) - 2)


def from_previous(value):
    return jnp.where(sublane_ids(value.shape) == 0, 0.0, pltpu.roll(value, 1, value.ndim - 2))


def from_next(value):
    return jnp.where(sublane_ids(value.shape) == CHUNKS - 1, 0.0, pltpu.roll(value, CHUNKS - 1, value.ndim - 2))


class Window:
    def __init__(self, make, count):
        self.make, self.count, self.known = make, count, {}

    def __call__(self, position):
        if position not in self.known:
            if position < 0:
                value = jax.tree.map(from_previous, self(position + self.count))
            elif position >= self.count:
                value = jax.tree.map(from_next, self(position - self.count))
            else:
                value = self.make(position)
            self.known[position] = value
        return self.known[position]


def local_solve(make_cells, make_viscous, count, part_ref, left_ref, right_ref, inner_ref, pay_ref, first_ref, last_ref):
    final, middle = count - 1, count // 2
    viscous = Window(make_viscous, count)
    face = functools.cache(lambda j: 0.5 * (viscous(j - 1) + viscous(j)))
    coupling = functools.cache(lambda j: ONE_THIRD - face(j))
    rows = lambda j: pl.ds(j * CHUNKS, CHUNKS)

    def diagonal(j):
        return 1.0 + face(j) + face(j + 1)

    inverse, tied, slope, reach = {}, {}, {}, {}
    for k in range(1, middle):
        for j, before, outer, inner in ((k, k - 1, k, k + 1), (final - k, final - k + 1, final - k + 1, final - k)):
            pivot = diagonal(j)
            if k > 1:
                pivot = pivot - coupling(outer) * slope[before]
            inverse[j] = 1.0 / pivot
            tied[j] = coupling(outer) * inverse[j]
            slope[j] = coupling(inner) * inverse[j]
            reach[j] = -tied[j] if k == 1 else -tied[j] * reach[before]
    low, high = middle - 1, middle
    meet = 1.0 / (1.0 - slope[low] * slope[high])
    left, right = {}, {}
    left[low], right[low] = reach[low] * meet, -(slope[low] * reach[high]) * meet
    left[high], right[high] = -slope[high] * left[low], reach[high] - slope[high] * right[low]
    for k in range(middle - 2, 0, -1):
        left[k], right[k] = reach[k] - slope[k] * left[k + 1], -slope[k] * right[k + 1]
        m = final - k
        left[m], right[m] = -slope[m] * left[m - 1], reach[m] - slope[m] * right[m - 1]
    for j in range(1, final):
        left_ref[:, rows(j), :] = left[j]
        right_ref[:, rows(j), :] = right[j]

    up_first, low_last = coupling(1), coupling(final)
    for h in range(2):
        cells = Window(functools.partial(make_cells, h), count)

        def source(j, q):
            u_low, u_mid, u_high = cells(j - 1)[0][q], cells(j)[0][q], cells(j + 1)[0][q]
            f = [cells(j + o)[1][q] for o in (-2, -1, 1, 2)]
            central = NEAR_WEIGHT * (f[2] - f[1]) + FAR_WEIGHT * (f[3] - f[0])
            return u_mid + ONE_THIRD * (u_low + u_high) - STEP_RATIO * central

        ends, carried = {}, {}
        for k in range(middle):
            for j, before in ((k, k - 1), (final - k, final - k + 1)):
                values = [source(j, q) for q in range(FIELDS)]
                if k == 0:
                    ends[j] = values
                    continue
                if k == 1:
                    carried[j] = [s * inverse[j][h] for s in values]
                else:
                    carried[j] = [s * inverse[j][h] - tied[j][h] * f for s, f in zip(values, carried[before])]
                if k < middle - 1:
                    for q in range(FIELDS):
                        part_ref[h, q, rows(j), :] = carried[j][q]
        solved_low = [(a - slope[low][h] * b) * meet[h] for a, b in zip(carried[low], carried[high])]
        solved_high = [b - slope[high][h] * a for a, b in zip(solved_low, carried[high])]
        for q in range(FIELDS):
            part_ref[h, q, rows(low), :] = solved_low[q]
            part_ref[h, q, rows(high), :] = solved_high[q]
        for k in range(middle - 2, 0, -1):
            solved_low = [part_ref[h, q, rows(k), :] - slope[k][h] * solved_low[q] for q in range(FIELDS)]
            m = final - k
            solved_high = [part_ref[h, q, rows(m), :] - slope[m][h] * solved_high[q] for q in range(FIELDS)]
            for q in range(FIELDS):
                part_ref[h, q, rows(k), :] = solved_low[q]
                part_ref[h, q, rows(m), :] = solved_high[q]
        for q in range(FIELDS):
            first_ref[h, pl.ds(q, CHUNKS, stride=8), :] = ends[0][q] - up_first[h] * solved_low[q]
            last_ref[h, pl.ds(q, CHUNKS, stride=8), :] = ends[final][q] - low_last[h] * solved_high[q]
            pay_ref[h, q : q + 1, :] = solved_low[q][0:1]
            pay_ref[h, 8 + q : 9 + q, :] = solved_high[q][CHUNKS - 1 : CHUNKS]
            pay_ref[h, ROW_RIGHT + q : ROW_RIGHT + q + 1, :] = ends[0][q][0:1]
            pay_ref[h, ROW_LEFT + q : ROW_LEFT + q + 1, :] = ends[final][q][CHUNKS - 1 : CHUNKS]
        zeros = jnp.zeros((CHUNKS, LANES), jnp.float32)
        ids = sublane_ids(zeros.shape)
        first_ref[h, pl.ds(5, CHUNKS, stride=8), :] = zeros
        first_ref[h, pl.ds(6, CHUNKS, stride=8), :] = jnp.where(ids == CHUNKS - 1, -up_first[h] * right[1][h], zeros)
        first_ref[h, pl.ds(7, CHUNKS, stride=8), :] = zeros
        last_ref[h, pl.ds(5, CHUNKS, stride=8), :] = jnp.where(ids == 0, -low_last[h] * left[final - 1][h], zeros)
        last_ref[h, pl.ds(6, CHUNKS, stride=8), :] = zeros
        last_ref[h, pl.ds(7, CHUNKS, stride=8), :] = zeros
        pay_ref[h, 5:6, :] = left[1][h][0:1]
        pay_ref[h, 6:8, :] = zeros[0:2]
        pay_ref[h, 13:14, :] = zeros[0:1]
        pay_ref[h, 14:15, :] = right[final - 1][h][CHUNKS - 1 : CHUNKS]
        pay_ref[h, 15:16, :] = zeros[0:1]

    def row(value, c):
        return value[:, c : c + 1, :]

    first_low, first_diag, first_up = coupling(0), diagonal(0) + up_first * left[1], up_first * right[1]
    last_low, last_diag = low_last * left[final - 1], diagonal(final) + low_last * right[final - 1]
    last_up = coupling(count)
    chain = []
    for c in range(CHUNKS):
        if c > 0:
            rhs = first_ref[:, 8 * c : 8 * c + 8, :]
            chain.append((row(first_low, c), row(first_diag, c), row(first_up, c), rhs))
        if c < CHUNKS - 1:
            rhs = last_ref[:, 8 * c : 8 * c + 8, :]
            chain.append((row(last_low, c), row(last_diag, c), row(last_up, c), rhs))
    solved = solve_chain(chain)
    inner_ref[:, 0:8, :] = jnp.zeros_like(solved[0])
    inner_ref[:, 120:128, :] = jnp.zeros_like(solved[0])
    for m, value in enumerate(solved):
        inner_ref[:, 8 * m + 8 : 8 * m + 16, :] = value

    eight = sublane_ids((2, 8, LANES))
    second = pay_ref[:, 0:8, :] + row(right[1], 0) * solved[0]
    end = pay_ref[:, ROW_RIGHT : ROW_RIGHT + 8, :]
    pay_ref[:, 0:8, :] = jnp.where(eight < FIELDS, end - row(up_first, 0) * second, second)
    second = pay_ref[:, 8:16, :] + row(left[final - 1], CHUNKS - 1) * solved[-1]
    end = pay_ref[:, ROW_LEFT : ROW_LEFT + 8, :]
    pay_ref[:, 8:16, :] = jnp.where(eight < FIELDS, end - row(low_last, CHUNKS - 1) * second, second)

    first = lambda value: value[..., 0:1, :]
    last = lambda value: value[..., CHUNKS - 1 : CHUNKS, :]
    pay_ref[:, 7:8, :] = first(viscous(0))
    pay_ref[:, 15:16, :] = last(viscous(final))
    pay_ref[:, ROW_HI : ROW_HI + 1, :] = first(face(1))
    pay_ref[:, ROW_LO : ROW_LO + 1, :] = last(face(final))
    pay_ref[:, 38:40, :] = jnp.zeros((2, 2, LANES), jnp.float32)
    for h in range(2):
        u_last, f_last = make_cells(h, final)
        f_before = make_cells(h, final - 1)[1]
        u_first, f_first = make_cells(h, 0)
        f_second = make_cells(h, 1)[1]
        for q in range(FIELDS):
            to_right = ONE_THIRD * u_last[q] + STEP_RATIO * (NEAR_WEIGHT * f_last[q] + FAR_WEIGHT * f_before[q])
            to_left = ONE_THIRD * u_first[q] - STEP_RATIO * (NEAR_WEIGHT * f_first[q] + FAR_WEIGHT * f_second[q])
            pay_ref[h, ROW_RIGHT + q : ROW_RIGHT + q + 1, :] = last(to_right)
            pay_ref[h, ROW_FLUX_RIGHT + q : ROW_FLUX_RIGHT + q + 1, :] = last(f_last[q])
            pay_ref[h, ROW_LEFT + q : ROW_LEFT + q + 1, :] = first(to_left)
            pay_ref[h, ROW_FLUX_LEFT + q : ROW_FLUX_LEFT + q + 1, :] = first(f_first[q])


def solve_chain(chain):
    size, middle = len(chain), len(chain) // 2
    slope, value = [None] * size, [None] * size
    for k in range(middle):
        for m, before in ((k, k - 1), (size - 1 - k, size - k)):
            low, diag, up, rhs = chain[m]
            outer, inner = (low, up) if m < middle else (up, low)
            if k > 0:
                diag = diag - outer * slope[before]
                rhs = rhs - outer * value[before]
            inverse = 1.0 / diag
            value[m] = rhs * inverse
            slope[m] = inner * inverse
    a, b = middle - 1, middle
    value[a] = (value[a] - slope[a] * value[b]) * (1.0 / (1.0 - slope[a] * slope[b]))
    value[b] = value[b] - slope[b] * value[a]
    for k in range(middle - 2, -1, -1):
        value[k] = value[k] - slope[k] * value[k + 1]
        m = size - 1 - k
        value[m] = value[m] - slope[m] * value[m - 1]
    return value


def reduced_solve(me, devices, all_ref, coef_ref, out_ref):
    def quantity(row):
        return jnp.stack(
            [all_ref[pl.ds(h * PAY_ROWS + row, devices, stride=2 * PAY_ROWS), :] for h in range(2)]
        )

    first_v, last_v = quantity(7), quantity(15)
    hi_first, lo_last = quantity(ROW_HI), quantity(ROW_LO)
    ids = sublane_ids(first_v.shape)
    at_start, at_end = ids == 0, ids == devices - 1
    v_below = jnp.where(at_start, 0.0, pltpu.roll(last_v, 1, 1))
    v_above = jnp.where(at_end, 0.0, pltpu.roll(first_v, devices - 1, 1))
    lo_first = 0.5 * (v_below + first_v)
    hi_last = 0.5 * (last_v + v_above)
    up_first = ONE_THIRD - hi_first
    low_last = ONE_THIRD - lo_last
    table = (
        jnp.where(at_start, 0.0, ONE_THIRD - lo_first),
        (1.0 + lo_first + hi_first) + up_first * quantity(5),
        up_first * quantity(6),
        low_last * quantity(13),
        (1.0 + lo_last + hi_last) + low_last * quantity(14),
        jnp.where(at_end, 0.0, ONE_THIRD - hi_last),
        1.0 / up_first,
        1.0 / low_last,
    )
    for i, value in enumerate(table):
        coef_ref[:, i * devices : (i + 1) * devices, :] = value

    def coef(i, d):
        return coef_ref[:, i * devices + d : i * devices + d + 1, :]

    def piece(d, row, size=8):
        return jnp.stack([all_ref[pl.ds((2 * d + h) * PAY_ROWS + row, size), :] for h in range(2)])

    def one(d, row):
        return piece(d, row, 1)

    chain, deltas = [], []
    for d in range(devices):
        rhs_first, rhs_last = piece(d, 0), piece(d, 8)
        delta_second = delta_before = None
        if d > 0:
            delta_second = FAR_SCALED * piece(d - 1, ROW_FLUX_RIGHT)
            rhs_first = rhs_first + piece(d - 1, ROW_RIGHT) + one(d, 5) * delta_second
            rhs_last = rhs_last + one(d, 6) * delta_second
        if d < devices - 1:
            delta_before = -FAR_SCALED * piece(d + 1, ROW_FLUX_LEFT)
            rhs_first = rhs_first + one(d, 13) * delta_before
            rhs_last = rhs_last + piece(d + 1, ROW_LEFT) + one(d, 14) * delta_before
        deltas.append((delta_second, delta_before))
        chain.append((coef(0, d), coef(1, d), coef(2, d), rhs_first))
        chain.append((coef(3, d), coef(4, d), coef(5, d), rhs_last))
    solved = solve_chain(chain)
    for d in range(devices):
        x_first, x_last = solved[2 * d], solved[2 * d + 1]
        delta_second, delta_before = deltas[d]
        seen_first = x_first if delta_second is None else x_first - delta_second * coef(6, d)
        seen_last = x_last if delta_before is None else x_last - delta_before * coef(7, d)
        for i, value in enumerate((x_first, x_last, seen_first, seen_last)):
            out_ref[:, d * 32 + 8 * i : d * 32 + 8 * i + 8, :] = value
    start = pl.multiple_of(me * 32, 32)
    mine = out_ref[:, pl.ds(start, 32), :]
    return [[mine[h, 8 * i : 8 * i + 8] for i in range(4)] for h in range(2)]


def rebuild(ends, count, part_ref, left_ref, right_ref, inner_ref, sol_ref, store):
    x_first, x_last, seen_first, seen_last = ends
    for m in range(16):
        if m == 0:
            value = seen_first
        elif m == 15:
            value = seen_last
        else:
            inner = inner_ref[8 * m : 8 * m + 8, :]
            value = inner + inner[5:6] * seen_first + inner[6:7] * seen_last
        sol_ref[8 * m : 8 * m + 8, :] = value
    chunk_first = [sol_ref[pl.ds(q, CHUNKS, stride=16), :] for q in range(FIELDS)]
    chunk_last = [sol_ref[pl.ds(8 + q, CHUNKS, stride=16), :] for q in range(FIELDS)]
    ids = sublane_ids(chunk_first[0].shape)
    for q in range(FIELDS):
        store(q, 0, jnp.where(ids == 0, x_first[q : q + 1], chunk_first[q]))
        store(q, count - 1, jnp.where(ids == CHUNKS - 1, x_last[q : q + 1], chunk_last[q]))
    for j in range(1, count - 1):
        left, right = left_ref[pl.ds(j * CHUNKS, CHUNKS), :], right_ref[pl.ds(j * CHUNKS, CHUNKS), :]
        for q in range(FIELDS):
            part = part_ref[q, pl.ds(j * CHUNKS, CHUNKS), :]
            store(q, j, part + left * chunk_first[q] + right * chunk_last[q])


def turn(from_ref, to_ref):
    for i in range(2):
        for k in range(2):
            to_ref[k, i * LANES : (i + 1) * LANES, :] = from_ref[i, k * LANES : (k + 1) * LANES, :].T


def lane_half(h):
    return pl.ds(h * LANES, LANES)


def x_kernel(
    count, state_ref, viscous_ref, part_ref, left_ref, right_ref, inner_ref, pay_ref, aux_ref,
    held_ref, first_ref, last_ref, sems,
):
    copies = [
        pltpu.make_async_copy(viscous_ref.at[:, lane_half(h)], held_ref.at[h, FIELDS], sems.at[h, FIELDS])
        for h in range(2)
    ] + [
        pltpu.make_async_copy(state_ref.at[q, :, lane_half(h)], held_ref.at[h, q], sems.at[h, q])
        for h in range(2)
        for q in range(FIELDS)
    ]
    for copy in copies:
        copy.start()
    for copy in copies:
        copy.wait()

    def make_cells(h, j):
        density, mom_x, mom_y, mom_z, energy = (strided(held_ref.at[h, q], j, count) for q in range(FIELDS))
        inverse = 1.0 / density
        vel_x = mom_x * inverse
        kinetic = mom_x * mom_x + mom_y * mom_y + mom_z * mom_z
        press = GAMMA_MINUS * (energy - 0.5 * kinetic * inverse)
        here = pl.ds(j * CHUNKS, CHUNKS)
        aux_ref[h, 0, here, :] = mom_y * inverse
        aux_ref[h, 1, here, :] = press
        flux = (mom_x, mom_x * vel_x + press, mom_y * vel_x, mom_z * vel_x, (energy + press) * vel_x)
        return (density, mom_x, mom_y, mom_z, energy), flux

    def make_viscous(j):
        value = jnp.stack([strided(held_ref.at[h, FIELDS], j, count) for h in range(2)])
        aux_ref[:, 2, pl.ds(j * CHUNKS, CHUNKS), :] = value
        return value

    local_solve(
        make_cells, make_viscous, count, part_ref, left_ref, right_ref, inner_ref, pay_ref, first_ref, last_ref
    )


def y_kernel(
    count, devices, devices_y, me_ref, all_ref, x_part_ref, x_left_ref, x_right_ref, x_inner_ref, aux_ref,
    part_ref, left_ref, right_ref, inner_ref, copies_ref,
    coef_ref, out_ref, sol_ref, section_ref, turned_ref, first_ref, last_ref, pay_ref, sems,
):
    ends = reduced_solve(me_ref[0] // devices_y, devices, all_ref, coef_ref, out_ref)
    for h in range(2):
        def store(q, j, value):
            section_ref[q, h, pl.ds(j * CHUNKS, CHUNKS), :] = value

        rebuild(
            ends[h], count, x_part_ref.at[h], x_left_ref.at[h], x_right_ref.at[h], x_inner_ref.at[h],
            sol_ref.at[h], store,
        )
    for i in range(3):
        turn(aux_ref.at[:, i], turned_ref.at[FIELDS + i])
    for q in range(FIELDS):
        turn(section_ref.at[q], turned_ref.at[q])

    def value(q, h, j):
        return strided(turned_ref.at[q, h], j, count)

    def make_cells(h, j):
        section = tuple(value(q, h, j) for q in range(FIELDS))
        vel_y, press = value(FIELDS, h, j), value(FIELDS + 1, h, j)
        flux = (
            vel_y * section[0], vel_y * section[1], vel_y * section[2] + press,
            vel_y * section[3], vel_y * section[4] + press * vel_y,
        )
        return section, flux

    def make_viscous(j):
        return jnp.stack([value(FIELDS + 2, h, j) for h in range(2)])

    local_solve(
        make_cells, make_viscous, count, part_ref, left_ref, right_ref, inner_ref, pay_ref, first_ref, last_ref
    )
    copies = [
        pltpu.make_async_copy(pay_ref, copies_ref.at[d], sems.at[d]) for d in range(copies_ref.shape[0])
    ]
    for copy in copies:
        copy.start()
    for copy in copies:
        copy.wait()


def last_kernel(
    count, devices, me_ref, all_ref, part_ref, left_ref, right_ref, inner_ref, new_ref,
    coef_ref, out_ref, sol_ref, section_ref, turned_ref, sems,
):
    ends = reduced_solve(lax.rem(me_ref[0], devices), devices, all_ref, coef_ref, out_ref)
    for h in range(2):
        def store(q, j, value):
            section_ref[q, h, pl.ds(j, CHUNKS, stride=count), :] = value

        rebuild(
            ends[h], count, part_ref.at[h], left_ref.at[h], right_ref.at[h], inner_ref.at[h], sol_ref.at[h], store
        )
    copies = []
    for q in range(FIELDS):
        turn(section_ref.at[q], turned_ref.at[q])
        for h in range(2):
            for c in range(CHUNKS):
                for k in range(count // 8):
                    rows = turned_ref[q, h, pl.ds(64 * k + c, 8, stride=CHUNKS), :]
                    section_ref[q, h, c * count + 8 * k : c * count + 8 * k + 8, :] = rows
            copies.append(
                pltpu.make_async_copy(section_ref.at[q, h], new_ref.at[q, :, lane_half(h)], sems.at[q, h])
            )
            copies[-1].start()
    for copy in copies:
        copy.wait()


def shards(devices_x, devices_y, state, viscous):
    cells = state.shape[2]
    count = cells // CHUNKS
    float_of = lambda *shape: jax.ShapeDtypeStruct(shape, jnp.float32)
    memory = lambda *shape: pltpu.VMEM(shape, jnp.float32)
    params = pltpu.CompilerParams(vmem_limit_bytes=48 * 1024 * 1024)
    whole = pl.BlockSpec(memory_space=pltpu.VMEM)
    far = pl.BlockSpec(memory_space=pltpu.HBM)
    scalar = pl.BlockSpec(memory_space=pltpu.SMEM)
    solved_shapes = [
        float_of(2, FIELDS, cells, LANES), float_of(2, cells, LANES), float_of(2, cells, LANES),
        float_of(2, 128, LANES),
    ]
    pay_shape = (2, PAY_ROWS, LANES)
    *x_parts, x_pay, aux = pl.pallas_call(
        functools.partial(x_kernel, count),
        out_shape=solved_shapes + [float_of(*pay_shape), float_of(2, 3, cells, LANES)],
        in_specs=[far] * 2,
        out_specs=[whole] * 6,
        scratch_shapes=[
            memory(2, FIELDS + 1, cells, LANES), memory(2, 64, LANES), memory(2, 64, LANES),
            pltpu.SemaphoreType.DMA((2, FIELDS + 1)),
        ],
        compiler_params=params,
        name="x_lines",
    )(
        pltpu.with_memory_space_constraint(state.reshape(FIELDS, cells, cells), pltpu.HBM),
        pltpu.with_memory_space_constraint(viscous.reshape(cells, cells), pltpu.HBM),
    )
    x_all = lax.all_gather(x_pay, "gx").reshape(devices_x * 2 * PAY_ROWS, LANES)
    me = (lax.axis_index("gx") * devices_y + lax.axis_index("gy")).astype(jnp.int32).reshape(1)

    def solve_scratch(devices):
        return [memory(2, 8 * devices, LANES), memory(2, 32 * devices, LANES), memory(2, 128, LANES)]

    *y_parts, copies = pl.pallas_call(
        functools.partial(y_kernel, count, devices_x, devices_y),
        out_shape=solved_shapes + [float_of(devices_y, *pay_shape)],
        in_specs=[scalar] + [whole] * 6,
        out_specs=[whole] * 4 + [far],
        scratch_shapes=solve_scratch(devices_x) + [
            memory(FIELDS, 2, cells, LANES), memory(FIELDS + 3, 2, cells, LANES),
            memory(2, 64, LANES), memory(2, 64, LANES), memory(*pay_shape),
            pltpu.SemaphoreType.DMA((devices_y,)),
        ],
        compiler_params=params,
        name="y_lines",
    )(me, x_all, *x_parts, aux)
    y_all = lax.all_to_all(copies, "gy", 0, 0).reshape(devices_y * 2 * PAY_ROWS, LANES)
    new = pl.pallas_call(
        functools.partial(last_kernel, count, devices_y),
        out_shape=float_of(FIELDS, cells, cells),
        in_specs=[scalar] + [whole] * 5,
        out_specs=far,
        scratch_shapes=solve_scratch(devices_y) + [
            memory(FIELDS, 2, cells, LANES), memory(FIELDS, 2, cells, LANES),
            pltpu.SemaphoreType.DMA((FIELDS, 2)),
        ],
        compiler_params=params,
        name="new_state",
    )(me, y_all, *y_parts)
    return new.reshape(state.shape)


def solution(mesh):
    placed = (P(None, None, "gx", "gy"), P(None, "gx", "gy"))
    return jax.shard_map(
        functools.partial(shards, mesh.shape["gx"], mesh.shape["gy"]),
        mesh=mesh, in_specs=placed, out_specs=P(None, None, "gx", "gy"), check_vma=False,
    )
```

```python
import functools
import jax
import jax.numpy as jnp
from jax import lax
from jax.experimental import pallas as pl
from jax.experimental.pallas import tpu as pltpu
from jax.sharding import PartitionSpec as P

STEP_RATIO = 0.25
ONE_THIRD = 1.0 / 3.0
NEAR_WEIGHT = 7.0 / 9.0
FAR_WEIGHT = 1.0 / 36.0
GAMMA_MINUS = 0.4
NEAR_SCALED = STEP_RATIO * NEAR_WEIGHT
FAR_RATIO = FAR_WEIGHT / NEAR_WEIGHT
FIELDS = 5
CHUNKS = 8
LANES = 128
PAY_ROWS = 40
ROW_RIGHT, ROW_HI, ROW_FLUX_RIGHT, ROW_LEFT, ROW_FLUX_LEFT, ROW_LO = 16, 21, 22, 27, 32, 37


def strided(ref, position, count):
    return ref[pl.ds(position, CHUNKS, stride=count), :]


def sublane_ids(shape):
    return lax.broadcasted_iota(jnp.int32, shape, len(shape) - 2)


def from_previous(value):
    return jnp.where(sublane_ids(value.shape) == 0, 0.0, pltpu.roll(value, 1, value.ndim - 2))


def from_next(value):
    return jnp.where(sublane_ids(value.shape) == CHUNKS - 1, 0.0, pltpu.roll(value, CHUNKS - 1, value.ndim - 2))


def local_solve(
    ready, make_terms, viscous_at, count, part_ref, left_ref, right_ref, inner_ref, pay_ref, first_ref, last_ref
):
    final, middle = count - 1, count // 2
    rows = lambda j: pl.ds(j * CHUNKS, CHUNKS)

    @functools.cache
    def viscous(j):
        if j < 0:
            return from_previous(viscous(j + count))
        if j >= count:
            return from_next(viscous(j - count))
        return viscous_at(j)

    face = functools.cache(lambda j: 0.5 * (viscous(j - 1) + viscous(j)))
    coupling = functools.cache(lambda j: ONE_THIRD - face(j))

    def diagonal(j):
        return 1.0 + face(j) + face(j + 1)

    inverse, tied, slope, reach = {}, {}, {}, {}
    for k in range(1, middle):
        for j, before, outer, inner in ((k, k - 1, k, k + 1), (final - k, final - k + 1, final - k + 1, final - k)):
            pivot = diagonal(j)
            if k > 1:
                pivot = pivot - coupling(outer) * slope[before]
            inverse[j] = 1.0 / pivot
            tied[j] = coupling(outer) * inverse[j]
            slope[j] = coupling(inner) * inverse[j]
            reach[j] = -tied[j] if k == 1 else -tied[j] * reach[before]
    low, high = middle - 1, middle
    meet = 1.0 / (1.0 - slope[low] * slope[high])
    left, right = {}, {}
    left[low], right[low] = reach[low] * meet, -(slope[low] * reach[high]) * meet
    left[high], right[high] = -slope[high] * left[low], reach[high] - slope[high] * right[low]
    for k in range(middle - 2, 0, -1):
        left[k], right[k] = reach[k] - slope[k] * left[k + 1], -slope[k] * right[k + 1]
        m = final - k
        left[m], right[m] = -slope[m] * left[m - 1], reach[m] - slope[m] * right[m - 1]
    for j in range(1, final):
        left_ref[:, rows(j), :] = left[j]
        right_ref[:, rows(j), :] = right[j]

    first = lambda value: value[..., 0:1, :]
    last = lambda value: value[..., CHUNKS - 1 : CHUNKS, :]
    up_first, low_last = coupling(1), coupling(final)
    fields = range(FIELDS)
    for h in range(2):
        ready(h)
        ends, carried = {}, None

        def take(j, sums):
            nonlocal carried
            if j == 0 or j == final:
                ends[j] = sums
                return
            if j == 1:
                carried = [s * inverse[j][h] for s in sums]
            elif j < middle:
                carried = [s * inverse[j][h] - tied[j][h] * f for s, f in zip(sums, carried)]
            for q in fields:
                part_ref[h, q, rows(j), :] = carried[q] if j < middle else sums[q]

        before, end = make_terms(h, final - 1), make_terms(h, final)
        for q in fields:
            pay_ref[h, ROW_RIGHT + q : ROW_RIGHT + q + 1, :] = last(end[q][2] + before[q][3])
            pay_ref[h, ROW_FLUX_RIGHT + q : ROW_FLUX_RIGHT + q + 1, :] = last(end[q][3])
        sums = {
            0: [from_previous(end[q][2] + before[q][3]) for q in fields],
            1: [from_previous(end[q][3]) for q in fields],
        }
        for j in range(count):
            terms = make_terms(h, j)
            if j == 0:
                zero = terms
            if j == 1:
                above_last = [from_next(zero[q][1] - terms[q][3]) for q in fields]
                above_before = [from_next(zero[q][3]) for q in fields]
                for q in fields:
                    to_left = first(zero[q][1] - terms[q][3])
                    pay_ref[h, ROW_LEFT + q : ROW_LEFT + q + 1, :] = to_left
                    pay_ref[h, ROW_FLUX_LEFT + q : ROW_FLUX_LEFT + q + 1, :] = -first(zero[q][3])
            if j >= 2:
                take(j - 2, [sums[j - 2][q] - terms[q][3] for q in fields])
                del sums[j - 2]
            if j >= 1:
                sums[j - 1] = [sums[j - 1][q] + terms[q][1] for q in fields]
            sums[j] = [sums[j][q] + terms[q][0] for q in fields]
            if j < final:
                if j == 0:
                    sums[1] = [sums[1][q] + terms[q][2] for q in fields]
                else:
                    sums[j + 1] = [sums[j + 1][q] + terms[q][2] for q in fields]
            if j < final - 1:
                sums[j + 2] = [terms[q][3] for q in fields]
        take(final - 1, [sums[final - 1][q] - above_before[q] for q in fields])
        take(final, [sums[final][q] + above_last[q] for q in fields])

        upper = None
        for j in range(final - 1, middle - 1, -1):
            values = [part_ref[h, q, rows(j), :] for q in fields]
            if upper is None:
                upper = [s * inverse[j][h] for s in values]
            else:
                upper = [s * inverse[j][h] - tied[j][h] * f for s, f in zip(values, upper)]
            if j > middle:
                for q in fields:
                    part_ref[h, q, rows(j), :] = upper[q]
        solved_low = [(a - slope[low][h] * b) * meet[h] for a, b in zip(carried, upper)]
        solved_high = [b - slope[high][h] * a for a, b in zip(solved_low, upper)]
        for q in fields:
            part_ref[h, q, rows(low), :] = solved_low[q]
            part_ref[h, q, rows(high), :] = solved_high[q]
        for k in range(middle - 2, 0, -1):
            solved_low = [part_ref[h, q, rows(k), :] - slope[k][h] * solved_low[q] for q in fields]
            m = final - k
            solved_high = [part_ref[h, q, rows(m), :] - slope[m][h] * solved_high[q] for q in fields]
            for q in fields:
                part_ref[h, q, rows(k), :] = solved_low[q]
                part_ref[h, q, rows(m), :] = solved_high[q]
        for q in fields:
            first_ref[h, pl.ds(q, CHUNKS, stride=8), :] = ends[0][q] - up_first[h] * solved_low[q]
            last_ref[h, pl.ds(q, CHUNKS, stride=8), :] = ends[final][q] - low_last[h] * solved_high[q]
            pay_ref[h, q : q + 1, :] = first(solved_low[q])
            pay_ref[h, 8 + q : 9 + q, :] = last(solved_high[q])
            first_ref[h, 64 + q : 65 + q, :] = first(ends[0][q])
            last_ref[h, 64 + q : 65 + q, :] = last(ends[final][q])
        zeros = jnp.zeros((CHUNKS, LANES), jnp.float32)
        ids = sublane_ids(zeros.shape)
        first_ref[h, pl.ds(5, CHUNKS, stride=8), :] = zeros
        first_ref[h, pl.ds(6, CHUNKS, stride=8), :] = jnp.where(ids == CHUNKS - 1, -up_first[h] * right[1][h], zeros)
        first_ref[h, pl.ds(7, CHUNKS, stride=8), :] = zeros
        last_ref[h, pl.ds(5, CHUNKS, stride=8), :] = jnp.where(ids == 0, -low_last[h] * left[final - 1][h], zeros)
        last_ref[h, pl.ds(6, CHUNKS, stride=8), :] = zeros
        last_ref[h, pl.ds(7, CHUNKS, stride=8), :] = zeros
        pay_ref[h, 5:6, :] = first(left[1][h])
        pay_ref[h, 6:8, :] = zeros[0:2]
        pay_ref[h, 13:14, :] = zeros[0:1]
        pay_ref[h, 14:15, :] = last(right[final - 1][h])
        pay_ref[h, 15:16, :] = zeros[0:1]

    def row(value, c):
        return value[:, c : c + 1, :]

    first_low, first_diag, first_up = coupling(0), diagonal(0) + up_first * left[1], up_first * right[1]
    last_low, last_diag = low_last * left[final - 1], diagonal(final) + low_last * right[final - 1]
    last_up = coupling(count)
    chain = []
    for c in range(CHUNKS):
        if c > 0:
            rhs = first_ref[:, 8 * c : 8 * c + 8, :]
            chain.append((row(first_low, c), row(first_diag, c), row(first_up, c), rhs))
        if c < CHUNKS - 1:
            rhs = last_ref[:, 8 * c : 8 * c + 8, :]
            chain.append((row(last_low, c), row(last_diag, c), row(last_up, c), rhs))
    solved = solve_chain(chain)
    inner_ref[:, 0:8, :] = jnp.zeros_like(solved[0])
    inner_ref[:, 120:128, :] = jnp.zeros_like(solved[0])
    for m, value in enumerate(solved):
        inner_ref[:, 8 * m + 8 : 8 * m + 16, :] = value

    eight = sublane_ids((2, 8, LANES))
    second = pay_ref[:, 0:8, :] + row(right[1], 0) * solved[0]
    pay_ref[:, 0:8, :] = jnp.where(eight < FIELDS, first_ref[:, 64:72, :] - row(up_first, 0) * second, second)
    second = pay_ref[:, 8:16, :] + row(left[final - 1], CHUNKS - 1) * solved[-1]
    pay_ref[:, 8:16, :] = jnp.where(
        eight < FIELDS, last_ref[:, 64:72, :] - row(low_last, CHUNKS - 1) * second, second
    )
    pay_ref[:, 7:8, :] = first(viscous(0))
    pay_ref[:, 15:16, :] = last(viscous(final))
    pay_ref[:, ROW_HI : ROW_HI + 1, :] = first(face(1))
    pay_ref[:, ROW_LO : ROW_LO + 1, :] = last(face(final))
    pay_ref[:, 38:40, :] = jnp.zeros((2, 2, LANES), jnp.float32)


def solve_chain(chain):
    size, middle = len(chain), len(chain) // 2
    slope, value = [None] * size, [None] * size
    for k in range(middle):
        for m, before in ((k, k - 1), (size - 1 - k, size - k)):
            low, diag, up, rhs = chain[m]
            outer, inner = (low, up) if m < middle else (up, low)
            if k > 0:
                diag = diag - outer * slope[before]
                rhs = rhs - outer * value[before]
            inverse = 1.0 / diag
            value[m] = rhs * inverse
            slope[m] = inner * inverse
    a, b = middle - 1, middle
    value[a] = (value[a] - slope[a] * value[b]) * (1.0 / (1.0 - slope[a] * slope[b]))
    value[b] = value[b] - slope[b] * value[a]
    for k in range(middle - 2, -1, -1):
        value[k] = value[k] - slope[k] * value[k + 1]
        m = size - 1 - k
        value[m] = value[m] - slope[m] * value[m - 1]
    return value


def reduced_solve(me, devices, all_ref, coef_ref, out_ref):
    def quantity(row):
        return jnp.stack(
            [all_ref[pl.ds(h * PAY_ROWS + row, devices, stride=2 * PAY_ROWS), :] for h in range(2)]
        )

    first_v, last_v = quantity(7), quantity(15)
    hi_first, lo_last = quantity(ROW_HI), quantity(ROW_LO)
    ids = sublane_ids(first_v.shape)
    at_start, at_end = ids == 0, ids == devices - 1
    v_below = jnp.where(at_start, 0.0, pltpu.roll(last_v, 1, 1))
    v_above = jnp.where(at_end, 0.0, pltpu.roll(first_v, devices - 1, 1))
    lo_first = 0.5 * (v_below + first_v)
    hi_last = 0.5 * (last_v + v_above)
    up_first = ONE_THIRD - hi_first
    low_last = ONE_THIRD - lo_last
    table = (
        jnp.where(at_start, 0.0, ONE_THIRD - lo_first),
        (1.0 + lo_first + hi_first) + up_first * quantity(5),
        up_first * quantity(6),
        low_last * quantity(13),
        (1.0 + lo_last + hi_last) + low_last * quantity(14),
        jnp.where(at_end, 0.0, ONE_THIRD - hi_last),
        1.0 / up_first,
        1.0 / low_last,
    )
    for i, value in enumerate(table):
        coef_ref[:, i * devices : (i + 1) * devices, :] = value

    def coef(i, d):
        return coef_ref[:, i * devices + d : i * devices + d + 1, :]

    def piece(d, row, size=8):
        return jnp.stack([all_ref[pl.ds((2 * d + h) * PAY_ROWS + row, size), :] for h in range(2)])

    def one(d, row):
        return piece(d, row, 1)

    chain, deltas = [], []
    for d in range(devices):
        rhs_first, rhs_last = piece(d, 0), piece(d, 8)
        delta_second = delta_before = None
        if d > 0:
            delta_second = piece(d - 1, ROW_FLUX_RIGHT)
            rhs_first = rhs_first + piece(d - 1, ROW_RIGHT) + one(d, 5) * delta_second
            rhs_last = rhs_last + one(d, 6) * delta_second
        if d < devices - 1:
            delta_before = piece(d + 1, ROW_FLUX_LEFT)
            rhs_first = rhs_first + one(d, 13) * delta_before
            rhs_last = rhs_last + piece(d + 1, ROW_LEFT) + one(d, 14) * delta_before
        deltas.append((delta_second, delta_before))
        chain.append((coef(0, d), coef(1, d), coef(2, d), rhs_first))
        chain.append((coef(3, d), coef(4, d), coef(5, d), rhs_last))
    solved = solve_chain(chain)
    for d in range(devices):
        x_first, x_last = solved[2 * d], solved[2 * d + 1]
        delta_second, delta_before = deltas[d]
        seen_first = x_first if delta_second is None else x_first - delta_second * coef(6, d)
        seen_last = x_last if delta_before is None else x_last - delta_before * coef(7, d)
        for i, value in enumerate((x_first, x_last, seen_first, seen_last)):
            out_ref[:, d * 32 + 8 * i : d * 32 + 8 * i + 8, :] = value
    start = pl.multiple_of(me * 32, 32)
    mine = out_ref[:, pl.ds(start, 32), :]
    return [[mine[h, 8 * i : 8 * i + 8] for i in range(4)] for h in range(2)]


def rebuild(ends, count, part_ref, left_ref, right_ref, inner_ref, sol_ref):
    x_first, x_last, seen_first, seen_last = ends
    for m in range(16):
        if m == 0:
            value = seen_first
        elif m == 15:
            value = seen_last
        else:
            inner = inner_ref[8 * m : 8 * m + 8, :]
            value = inner + inner[5:6] * seen_first + inner[6:7] * seen_last
        sol_ref[8 * m : 8 * m + 8, :] = value
    chunk_first = [sol_ref[pl.ds(q, CHUNKS, stride=16), :] for q in range(FIELDS)]
    chunk_last = [sol_ref[pl.ds(8 + q, CHUNKS, stride=16), :] for q in range(FIELDS)]
    ids = sublane_ids(chunk_first[0].shape)

    def solution_at(q, j):
        if j == 0:
            return jnp.where(ids == 0, x_first[q : q + 1], chunk_first[q])
        if j == count - 1:
            return jnp.where(ids == CHUNKS - 1, x_last[q : q + 1], chunk_last[q])
        here = pl.ds(j * CHUNKS, CHUNKS)
        return part_ref[q, here, :] + left_ref[here, :] * chunk_first[q] + right_ref[here, :] * chunk_last[q]

    return solution_at


def turn(count, from_ref, to_ref):
    for k in range(2):
        starts = [64 * t + c for c in range(4 * k, 4 * k + 4) for t in range(count // 8)]
        for i in range(2):
            tiles = [from_ref[i, pl.ds(start, 8, stride=CHUNKS), :] for start in starts]
            to_ref[k, i * LANES : (i + 1) * LANES, :] = jnp.concatenate(tiles, 0).T


def lane_half(h):
    return pl.ds(h * LANES, LANES)


def x_kernel(
    count, state_ref, viscous_ref, part_ref, left_ref, right_ref, inner_ref, pay_ref, aux_ref,
    held_ref, first_ref, last_ref, sems,
):
    copies = [
        pltpu.make_async_copy(viscous_ref.at[:, lane_half(h)], held_ref.at[h, FIELDS], sems.at[h, FIELDS])
        for h in range(2)
    ] + [
        pltpu.make_async_copy(state_ref.at[q, :, lane_half(h)], held_ref.at[h, q], sems.at[h, q])
        for h in range(2)
        for q in range(FIELDS)
    ]
    for copy in copies:
        copy.start()
    for copy in copies[:2]:
        copy.wait()

    def ready(h):
        for copy in copies[2 + FIELDS * h : 2 + FIELDS * (h + 1)]:
            copy.wait()

    def make_terms(h, j):
        density, mom_x, mom_y, mom_z, energy = (strided(held_ref.at[h, q], j, count) for q in range(FIELDS))
        inverse = 1.0 / density
        vel_x = (NEAR_SCALED * inverse) * mom_x
        kinetic = mom_x * mom_x + mom_y * mom_y + mom_z * mom_z
        press = GAMMA_MINUS * (energy - 0.5 * kinetic * inverse)
        here = pl.ds(j * CHUNKS, CHUNKS)
        aux_ref[h, 0, here, :] = (NEAR_SCALED * inverse) * mom_y
        aux_ref[h, 1, here, :] = press
        low, high, far = ONE_THIRD - vel_x, ONE_THIRD + vel_x, FAR_RATIO * vel_x

        def general(u, flux):
            third = ONE_THIRD * u
            return u, third - flux, third + flux, FAR_RATIO * flux

        def carried(u):
            return u, low * u, high * u, far * u

        return (
            general(density, NEAR_SCALED * mom_x),
            general(mom_x, mom_x * vel_x + NEAR_SCALED * press),
            carried(mom_y),
            carried(mom_z),
            general(energy, (energy + press) * vel_x),
        )

    def viscous_at(j):
        value = jnp.stack([strided(held_ref.at[h, FIELDS], j, count) for h in range(2)])
        aux_ref[:, 2, pl.ds(j * CHUNKS, CHUNKS), :] = value
        return value

    local_solve(
        ready, make_terms, viscous_at, count, part_ref, left_ref, right_ref, inner_ref, pay_ref, first_ref, last_ref
    )


def y_kernel(
    count, devices, devices_y, me_ref, all_ref, x_part_ref, x_left_ref, x_right_ref, x_inner_ref, aux_ref,
    part_ref, left_ref, right_ref, inner_ref, copies_ref,
    coef_ref, out_ref, sol_ref, section_ref, turned_ref, first_ref, last_ref, pay_ref, sems,
):
    ends = reduced_solve(me_ref[0] // devices_y, devices, all_ref, coef_ref, out_ref)
    for i in range(3):
        turn(count, aux_ref.at[:, i], turned_ref.at[FIELDS + i])
    halves = [
        rebuild(
            ends[h], count, x_part_ref.at[h], x_left_ref.at[h], x_right_ref.at[h], x_inner_ref.at[h], sol_ref.at[h]
        )
        for h in range(2)
    ]
    for q in range(FIELDS):
        for h in range(2):
            for j in range(count):
                section_ref[q, h, pl.ds(j * CHUNKS, CHUNKS), :] = halves[h](q, j)
        turn(count, section_ref.at[q], turned_ref.at[q])

    def value(q, h, j):
        return strided(turned_ref.at[q, h], j, count)

    def make_terms(h, j):
        vel_y, press = value(FIELDS, h, j), value(FIELDS + 1, h, j)
        low, high, far = ONE_THIRD - vel_y, ONE_THIRD + vel_y, FAR_RATIO * vel_y

        def carried(u):
            return u, low * u, high * u, far * u

        def pressed(u, flux):
            return u, low * u - flux, high * u + flux, far * u + FAR_RATIO * flux

        return (
            carried(value(0, h, j)),
            carried(value(1, h, j)),
            pressed(value(2, h, j), NEAR_SCALED * press),
            carried(value(3, h, j)),
            pressed(value(4, h, j), press * vel_y),
        )

    def viscous_at(j):
        return jnp.stack([value(FIELDS + 2, h, j) for h in range(2)])

    local_solve(
        lambda h: None, make_terms, viscous_at, count,
        part_ref, left_ref, right_ref, inner_ref, pay_ref, first_ref, last_ref,
    )
    copies = [
        pltpu.make_async_copy(pay_ref, copies_ref.at[d], sems.at[d]) for d in range(copies_ref.shape[0])
    ]
    for copy in copies:
        copy.start()
    for copy in copies:
        copy.wait()


def last_kernel(
    count, devices, me_ref, all_ref, part_ref, left_ref, right_ref, inner_ref, new_ref,
    coef_ref, out_ref, sol_ref, section_ref, turned_ref, sems,
):
    ends = reduced_solve(lax.rem(me_ref[0], devices), devices, all_ref, coef_ref, out_ref)
    halves = [
        rebuild(ends[h], count, part_ref.at[h], left_ref.at[h], right_ref.at[h], inner_ref.at[h], sol_ref.at[h])
        for h in range(2)
    ]
    copies = []
    for q in range(FIELDS):
        for h in range(2):
            for j in range(count):
                section_ref[q, h, pl.ds(j * CHUNKS, CHUNKS), :] = halves[h](q, j)
        turn(count, section_ref.at[q], turned_ref.at[q])
        for h in range(2):
            copies.append(
                pltpu.make_async_copy(turned_ref.at[q, h], new_ref.at[q, :, lane_half(h)], sems.at[q, h])
            )
            copies[-1].start()
    for copy in copies:
        copy.wait()


def shards(devices_x, devices_y, state, viscous):
    cells = state.shape[2]
    count = cells // CHUNKS
    float_of = lambda *shape: jax.ShapeDtypeStruct(shape, jnp.float32)
    memory = lambda *shape: pltpu.VMEM(shape, jnp.float32)
    params = pltpu.CompilerParams(vmem_limit_bytes=48 * 1024 * 1024)
    whole = pl.BlockSpec(memory_space=pltpu.VMEM)
    far = pl.BlockSpec(memory_space=pltpu.HBM)
    scalar = pl.BlockSpec(memory_space=pltpu.SMEM)
    solved_shapes = [
        float_of(2, FIELDS, cells, LANES), float_of(2, cells, LANES), float_of(2, cells, LANES),
        float_of(2, 128, LANES),
    ]
    pay_shape = (2, PAY_ROWS, LANES)
    *x_parts, x_pay, aux = pl.pallas_call(
        functools.partial(x_kernel, count),
        out_shape=solved_shapes + [float_of(*pay_shape), float_of(2, 3, cells, LANES)],
        in_specs=[far] * 2,
        out_specs=[whole] * 6,
        scratch_shapes=[
            memory(2, FIELDS + 1, cells, LANES), memory(2, 72, LANES), memory(2, 72, LANES),
            pltpu.SemaphoreType.DMA((2, FIELDS + 1)),
        ],
        compiler_params=params,
        name="x_lines",
    )(
        pltpu.with_memory_space_constraint(state.reshape(FIELDS, cells, cells), pltpu.HBM),
        pltpu.with_memory_space_constraint(viscous.reshape(cells, cells), pltpu.HBM),
    )
    x_all = lax.all_gather(x_pay, "gx").reshape(devices_x * 2 * PAY_ROWS, LANES)
    me = (lax.axis_index("gx") * devices_y + lax.axis_index("gy")).astype(jnp.int32).reshape(1)

    def solve_scratch(devices):
        return [memory(2, 8 * devices, LANES), memory(2, 32 * devices, LANES), memory(2, 128, LANES)]

    *y_parts, copies = pl.pallas_call(
        functools.partial(y_kernel, count, devices_x, devices_y),
        out_shape=solved_shapes + [float_of(devices_y, *pay_shape)],
        in_specs=[scalar] + [whole] * 6,
        out_specs=[whole] * 4 + [far],
        scratch_shapes=solve_scratch(devices_x) + [
            memory(FIELDS, 2, cells, LANES), memory(FIELDS + 3, 2, cells, LANES),
            memory(2, 72, LANES), memory(2, 72, LANES), memory(*pay_shape),
            pltpu.SemaphoreType.DMA((devices_y,)),
        ],
        compiler_params=params,
        name="y_lines",
    )(me, x_all, *x_parts, aux)
    y_all = lax.all_to_all(copies, "gy", 0, 0).reshape(devices_y * 2 * PAY_ROWS, LANES)
    new = pl.pallas_call(
        functools.partial(last_kernel, count, devices_y),
        out_shape=float_of(FIELDS, cells, cells),
        in_specs=[scalar] + [whole] * 5,
        out_specs=far,
        scratch_shapes=solve_scratch(devices_y) + [
            memory(FIELDS, 2, cells, LANES), memory(FIELDS, 2, cells, LANES),
            pltpu.SemaphoreType.DMA((FIELDS, 2)),
        ],
        compiler_params=params,
        name="new_state",
    )(me, y_all, *y_parts)
    return new.reshape(state.shape)


def solution(mesh):
    placed = (P(None, None, "gx", "gy"), P(None, "gx", "gy"))
    return jax.shard_map(
        functools.partial(shards, mesh.shape["gx"], mesh.shape["gy"]),
        mesh=mesh, in_specs=placed, out_specs=P(None, None, "gx", "gy"), check_vma=False,
    )
```

```python
import functools
import jax
import jax.numpy as jnp
from jax import lax
from jax.experimental import pallas as pl
from jax.experimental.pallas import tpu as pltpu
from jax.sharding import PartitionSpec as P

STEP_RATIO = 0.25
ONE_THIRD = 1.0 / 3.0
NEAR_WEIGHT = 7.0 / 9.0
FAR_WEIGHT = 1.0 / 36.0
GAMMA_MINUS = 0.4
NEAR_SCALED = STEP_RATIO * NEAR_WEIGHT
FAR_RATIO = FAR_WEIGHT / NEAR_WEIGHT
FIELDS = 5
CHUNKS = 8
LANES = 128
PAY_ROWS = 40
ROW_RIGHT, ROW_HI, ROW_FLUX_RIGHT, ROW_LEFT, ROW_FLUX_LEFT, ROW_LO = 16, 21, 22, 27, 32, 37


def strided(ref, position, count):
    return ref[pl.ds(position, CHUNKS, stride=count), :]


def sublane_ids(shape):
    return lax.broadcasted_iota(jnp.int32, shape, len(shape) - 2)


def from_previous(value):
    return jnp.where(sublane_ids(value.shape) == 0, 0.0, pltpu.roll(value, 1, value.ndim - 2))


def from_next(value):
    return jnp.where(sublane_ids(value.shape) == CHUNKS - 1, 0.0, pltpu.roll(value, CHUNKS - 1, value.ndim - 2))


def local_solve(
    ready, make_terms, viscous_at, count, part_ref, left_ref, right_ref, inner_ref, pay_ref, first_ref, last_ref
):
    final, middle = count - 1, count // 2
    rows = lambda j: pl.ds(j * CHUNKS, CHUNKS)

    @functools.cache
    def viscous(j):
        if j < 0:
            return from_previous(viscous(j + count))
        if j >= count:
            return from_next(viscous(j - count))
        return viscous_at(j)

    face = functools.cache(lambda j: 0.5 * (viscous(j - 1) + viscous(j)))
    coupling = functools.cache(lambda j: ONE_THIRD - face(j))

    def diagonal(j):
        return 1.0 + face(j) + face(j + 1)

    inverse, tied, slope, reach = {}, {}, {}, {}
    for k in range(1, middle):
        for j, before, outer, inner in ((k, k - 1, k, k + 1), (final - k, final - k + 1, final - k + 1, final - k)):
            pivot = diagonal(j)
            if k > 1:
                pivot = pivot - coupling(outer) * slope[before]
            inverse[j] = 1.0 / pivot
            tied[j] = coupling(outer) * inverse[j]
            slope[j] = coupling(inner) * inverse[j]
            reach[j] = -tied[j] if k == 1 else -tied[j] * reach[before]
    low, high = middle - 1, middle
    meet = 1.0 / (1.0 - slope[low] * slope[high])
    left, right = {}, {}
    left[low], right[low] = reach[low] * meet, -(slope[low] * reach[high]) * meet
    left[high], right[high] = -slope[high] * left[low], reach[high] - slope[high] * right[low]
    for k in range(middle - 2, 0, -1):
        left[k], right[k] = reach[k] - slope[k] * left[k + 1], -slope[k] * right[k + 1]
        m = final - k
        left[m], right[m] = -slope[m] * left[m - 1], reach[m] - slope[m] * right[m - 1]
    for j in range(1, final):
        left_ref[:, rows(j), :] = left[j]
        right_ref[:, rows(j), :] = right[j]

    first = lambda value: value[..., 0:1, :]
    last = lambda value: value[..., CHUNKS - 1 : CHUNKS, :]
    up_first, low_last = coupling(1), coupling(final)
    fields = range(FIELDS)
    for h in range(2):
        ready(h)
        ends, carried = {}, None

        def take(j, sums):
            nonlocal carried
            if j == 0 or j == final:
                ends[j] = sums
                return
            if j == 1:
                carried = [s * inverse[j][h] for s in sums]
            elif j < middle:
                carried = [s * inverse[j][h] - tied[j][h] * f for s, f in zip(sums, carried)]
            for q in fields:
                part_ref[h, q, rows(j), :] = carried[q] if j < middle else sums[q]

        before, end = make_terms(h, final - 1), make_terms(h, final)
        for q in fields:
            pay_ref[h, ROW_RIGHT + q : ROW_RIGHT + q + 1, :] = last(end[q][2] + before[q][3])
            pay_ref[h, ROW_FLUX_RIGHT + q : ROW_FLUX_RIGHT + q + 1, :] = last(end[q][3])
        sums = {
            0: [from_previous(end[q][2] + before[q][3]) for q in fields],
            1: [from_previous(end[q][3]) for q in fields],
        }
        for j in range(count):
            terms = make_terms(h, j)
            if j == 0:
                zero = terms
            if j == 1:
                above_last = [from_next(zero[q][1] - terms[q][3]) for q in fields]
                above_before = [from_next(zero[q][3]) for q in fields]
                for q in fields:
                    to_left = first(zero[q][1] - terms[q][3])
                    pay_ref[h, ROW_LEFT + q : ROW_LEFT + q + 1, :] = to_left
                    pay_ref[h, ROW_FLUX_LEFT + q : ROW_FLUX_LEFT + q + 1, :] = -first(zero[q][3])
            if j >= 2:
                take(j - 2, [sums[j - 2][q] - terms[q][3] for q in fields])
                del sums[j - 2]
            if j >= 1:
                sums[j - 1] = [sums[j - 1][q] + terms[q][1] for q in fields]
            sums[j] = [sums[j][q] + terms[q][0] for q in fields]
            if j < final:
                if j == 0:
                    sums[1] = [sums[1][q] + terms[q][2] for q in fields]
                else:
                    sums[j + 1] = [sums[j + 1][q] + terms[q][2] for q in fields]
            if j < final - 1:
                sums[j + 2] = [terms[q][3] for q in fields]
        take(final - 1, [sums[final - 1][q] - above_before[q] for q in fields])
        take(final, [sums[final][q] + above_last[q] for q in fields])

        upper = None
        for j in range(final - 1, middle - 1, -1):
            values = [part_ref[h, q, rows(j), :] for q in fields]
            if upper is None:
                upper = [s * inverse[j][h] for s in values]
            else:
                upper = [s * inverse[j][h] - tied[j][h] * f for s, f in zip(values, upper)]
            if j > middle:
                for q in fields:
                    part_ref[h, q, rows(j), :] = upper[q]
        solved_low = [(a - slope[low][h] * b) * meet[h] for a, b in zip(carried, upper)]
        solved_high = [b - slope[high][h] * a for a, b in zip(solved_low, upper)]
        for q in fields:
            part_ref[h, q, rows(low), :] = solved_low[q]
            part_ref[h, q, rows(high), :] = solved_high[q]
        for k in range(middle - 2, 0, -1):
            solved_low = [part_ref[h, q, rows(k), :] - slope[k][h] * solved_low[q] for q in fields]
            m = final - k
            solved_high = [part_ref[h, q, rows(m), :] - slope[m][h] * solved_high[q] for q in fields]
            for q in fields:
                part_ref[h, q, rows(k), :] = solved_low[q]
                part_ref[h, q, rows(m), :] = solved_high[q]
        for q in fields:
            first_ref[h, pl.ds(q, CHUNKS, stride=8), :] = ends[0][q] - up_first[h] * solved_low[q]
            last_ref[h, pl.ds(q, CHUNKS, stride=8), :] = ends[final][q] - low_last[h] * solved_high[q]
            pay_ref[h, q : q + 1, :] = first(solved_low[q])
            pay_ref[h, 8 + q : 9 + q, :] = last(solved_high[q])
            first_ref[h, 64 + q : 65 + q, :] = first(ends[0][q])
            last_ref[h, 64 + q : 65 + q, :] = last(ends[final][q])
        zeros = jnp.zeros((CHUNKS, LANES), jnp.float32)
        ids = sublane_ids(zeros.shape)
        first_ref[h, pl.ds(5, CHUNKS, stride=8), :] = zeros
        first_ref[h, pl.ds(6, CHUNKS, stride=8), :] = jnp.where(ids == CHUNKS - 1, -up_first[h] * right[1][h], zeros)
        first_ref[h, pl.ds(7, CHUNKS, stride=8), :] = zeros
        last_ref[h, pl.ds(5, CHUNKS, stride=8), :] = jnp.where(ids == 0, -low_last[h] * left[final - 1][h], zeros)
        last_ref[h, pl.ds(6, CHUNKS, stride=8), :] = zeros
        last_ref[h, pl.ds(7, CHUNKS, stride=8), :] = zeros
        pay_ref[h, 5:6, :] = first(left[1][h])
        pay_ref[h, 6:8, :] = zeros[0:2]
        pay_ref[h, 13:14, :] = zeros[0:1]
        pay_ref[h, 14:15, :] = last(right[final - 1][h])
        pay_ref[h, 15:16, :] = zeros[0:1]

    def row(value, c):
        return value[:, c : c + 1, :]

    first_low, first_diag, first_up = coupling(0), diagonal(0) + up_first * left[1], up_first * right[1]
    last_low, last_diag = low_last * left[final - 1], diagonal(final) + low_last * right[final - 1]
    last_up = coupling(count)
    chain = []
    for c in range(CHUNKS):
        if c > 0:
            rhs = first_ref[:, 8 * c : 8 * c + 8, :]
            chain.append((row(first_low, c), row(first_diag, c), row(first_up, c), rhs))
        if c < CHUNKS - 1:
            rhs = last_ref[:, 8 * c : 8 * c + 8, :]
            chain.append((row(last_low, c), row(last_diag, c), row(last_up, c), rhs))
    solved = solve_chain(chain)
    inner_ref[:, 0:8, :] = jnp.zeros_like(solved[0])
    inner_ref[:, 120:128, :] = jnp.zeros_like(solved[0])
    for m, value in enumerate(solved):
        inner_ref[:, 8 * m + 8 : 8 * m + 16, :] = value

    eight = sublane_ids((2, 8, LANES))
    second = pay_ref[:, 0:8, :] + row(right[1], 0) * solved[0]
    pay_ref[:, 0:8, :] = jnp.where(eight < FIELDS, first_ref[:, 64:72, :] - row(up_first, 0) * second, second)
    second = pay_ref[:, 8:16, :] + row(left[final - 1], CHUNKS - 1) * solved[-1]
    pay_ref[:, 8:16, :] = jnp.where(
        eight < FIELDS, last_ref[:, 64:72, :] - row(low_last, CHUNKS - 1) * second, second
    )
    pay_ref[:, 7:8, :] = first(viscous(0))
    pay_ref[:, 15:16, :] = last(viscous(final))
    pay_ref[:, ROW_HI : ROW_HI + 1, :] = first(face(1))
    pay_ref[:, ROW_LO : ROW_LO + 1, :] = last(face(final))
    pay_ref[:, 38:40, :] = jnp.zeros((2, 2, LANES), jnp.float32)


def solve_chain(chain):
    size, middle = len(chain), len(chain) // 2
    slope, value = [None] * size, [None] * size
    for k in range(middle):
        for m, before in ((k, k - 1), (size - 1 - k, size - k)):
            low, diag, up, rhs = chain[m]
            outer, inner = (low, up) if m < middle else (up, low)
            if k > 0:
                diag = diag - outer * slope[before]
                rhs = rhs - outer * value[before]
            inverse = 1.0 / diag
            value[m] = rhs * inverse
            slope[m] = inner * inverse
    a, b = middle - 1, middle
    value[a] = (value[a] - slope[a] * value[b]) * (1.0 / (1.0 - slope[a] * slope[b]))
    value[b] = value[b] - slope[b] * value[a]
    for k in range(middle - 2, -1, -1):
        value[k] = value[k] - slope[k] * value[k + 1]
        m = size - 1 - k
        value[m] = value[m] - slope[m] * value[m - 1]
    return value


def join(blocks, at_ends):
    count = len(blocks)
    one = lambda b, row: blocks[b](row, 1)
    face = lambda b: 0.5 * (one(b, 15) + one(b + 1, 7))
    chain, deltas, scales = [], [], []
    for b in range(count):
        rhs_first, rhs_last = blocks[b](0, 8), blocks[b](8, 8)
        second = before = None
        if b > 0:
            second = blocks[b - 1](ROW_FLUX_RIGHT, 8)
            rhs_first = rhs_first + blocks[b - 1](ROW_RIGHT, 8) + one(b, 5) * second
            rhs_last = rhs_last + one(b, 6) * second
        if b < count - 1:
            before = blocks[b + 1](ROW_FLUX_LEFT, 8)
            rhs_first = rhs_first + one(b, 13) * before
            rhs_last = rhs_last + blocks[b + 1](ROW_LEFT, 8) + one(b, 14) * before
        up, low = ONE_THIRD - one(b, ROW_HI), ONE_THIRD - one(b, ROW_LO)
        lo_first = face(b - 1) if b > 0 else 0.5 * one(b, 7)
        hi_last = face(b) if b < count - 1 else 0.5 * one(b, 15)
        zero = jnp.zeros_like(up)
        outer_low = ONE_THIRD - lo_first if b > 0 else zero
        outer_up = ONE_THIRD - hi_last if b < count - 1 else zero
        chain.append((outer_low, (1.0 + lo_first + one(b, ROW_HI)) + up * one(b, 5), up * one(b, 6), rhs_first))
        chain.append((low * one(b, 13), (1.0 + one(b, ROW_LO) + hi_last) + low * one(b, 14), outer_up, rhs_last))
        deltas.append((second, before))
        scales.append((up, low))
    return chain if at_ends else chain[1:-1], chain[0], chain[-1], deltas, scales


def ordered(place, pay_refs, blocks_ref):
    for k, pay_ref in enumerate(pay_refs):
        blocks_ref[jnp.bitwise_xor(place, k)] = pay_ref[...]
    return [lambda row, size, b=b: blocks_ref[b, :, row : row + size, :] for b in range(len(pay_refs))]


def place_in(stage, me_ref):
    first, size, _ = stage
    return lax.rem(me_ref[0] // first, size)


def merge_kernel(stage, me_ref, *refs):
    size = stage[1]
    pay_refs, (merged_ref, own_ref, blocks_ref, table_ref) = refs[:size], refs[size:]
    place = place_in(stage, me_ref)
    blocks = ordered(place, pay_refs, blocks_ref)
    chain, first, last, deltas, scales = join(blocks, False)
    eight = sublane_ids((2, 8, LANES))
    is_field = eight < FIELDS
    rhs = [jnp.where(is_field, value, 0.0) for _, _, _, value in chain]
    rhs[0] = jnp.where(eight == 5, -chain[0][0], rhs[0])
    rhs[-1] = jnp.where(eight == 6, -chain[-1][2], rhs[-1])
    inner = solve_chain([(low, diag, up, value) for (low, diag, up, _), value in zip(chain, rhs)])

    merged_ref[:, 0:8, :] = first[3] - first[2] * inner[0]
    merged_ref[:, 8:16, :] = last[3] - last[0] * inner[-1]
    merged_ref[:, 5:6, :] = blocks[0](5, 1) + blocks[0](6, 1) * inner[0][:, 5:6, :]
    merged_ref[:, 6:7, :] = blocks[0](6, 1) * inner[0][:, 6:7, :]
    merged_ref[:, 7:8, :] = blocks[0](7, 1)
    merged_ref[:, 13:14, :] = blocks[-1](13, 1) * inner[-1][:, 5:6, :]
    merged_ref[:, 14:15, :] = blocks[-1](14, 1) + blocks[-1](13, 1) * inner[-1][:, 6:7, :]
    merged_ref[:, 15:16, :] = blocks[-1](15, 1)
    for row, rows, block in (
        (ROW_RIGHT, 5, -1), (ROW_HI, 1, 0), (ROW_FLUX_RIGHT, 5, -1), (ROW_LEFT, 10, 0), (ROW_LO, 1, -1)
    ):
        merged_ref[:, row : row + rows, :] = blocks[block](row, rows)
    merged_ref[:, 38:40, :] = jnp.zeros((2, 2, LANES), jnp.float32)

    for b in range(size):
        zero = jnp.zeros((2, 8, LANES), jnp.float32)
        own_first = jnp.where((eight == 5) | (eight == 7), 1.0, zero) if b == 0 else inner[2 * b - 1]
        own_last = jnp.where((eight == 6) | (eight == 7), 1.0, zero) if b == size - 1 else inner[2 * b]
        second, before = deltas[b]
        second = zero if second is None else jnp.where(is_field, second / scales[b][0], 0.0)
        before = zero if before is None else jnp.where(is_field, before / scales[b][1], 0.0)
        for i, value in enumerate((own_first, own_last, second, before)):
            table_ref[:, b * 32 + 8 * i : b * 32 + 8 * i + 8, :] = value
    own_ref[...] = table_ref[:, pl.ds(pl.multiple_of(place * 32, 32), 32), :]


def outer_solve(stage, me_ref, pay_refs, own_refs, blocks_ref, table_ref):
    place = place_in(stage, me_ref)
    chain, _, _, deltas, scales = join(ordered(place, pay_refs, blocks_ref), True)
    solved = solve_chain(chain)
    for b in range(stage[1]):
        x_first, x_last = solved[2 * b], solved[2 * b + 1]
        second, before = deltas[b]
        seen_first = x_first if second is None else x_first - second / scales[b][0]
        seen_last = x_last if before is None else x_last - before / scales[b][1]
        for i, value in enumerate((x_first, x_last, seen_first, seen_last)):
            table_ref[:, b * 32 + 8 * i : b * 32 + 8 * i + 8, :] = value
    mine = table_ref[:, pl.ds(pl.multiple_of(place * 32, 32), 32), :]
    ends = [mine[:, 8 * i : 8 * i + 8] for i in range(4)]
    for own_ref in own_refs:
        x_first, x_last, seen_first, seen_last = ends
        own_first, own_last, second, before = (own_ref[:, 8 * i : 8 * i + 8, :] for i in range(4))
        first = own_first + own_first[:, 5:6] * seen_first + own_first[:, 6:7] * seen_last
        last = own_last + own_last[:, 5:6] * seen_first + own_last[:, 6:7] * seen_last
        ends = [
            first + own_first[:, 7:8] * (x_first - seen_first),
            last + own_last[:, 7:8] * (x_last - seen_last),
            first - second,
            last - before,
        ]
    return [[value[h] for value in ends] for h in range(2)]


def rebuild(ends, count, part_ref, left_ref, right_ref, inner_ref, sol_ref):
    x_first, x_last, seen_first, seen_last = ends
    for m in range(16):
        if m == 0:
            value = seen_first
        elif m == 15:
            value = seen_last
        else:
            inner = inner_ref[8 * m : 8 * m + 8, :]
            value = inner + inner[5:6] * seen_first + inner[6:7] * seen_last
        sol_ref[8 * m : 8 * m + 8, :] = value
    chunk_first = [sol_ref[pl.ds(q, CHUNKS, stride=16), :] for q in range(FIELDS)]
    chunk_last = [sol_ref[pl.ds(8 + q, CHUNKS, stride=16), :] for q in range(FIELDS)]
    ids = sublane_ids(chunk_first[0].shape)

    def solution_at(q, j):
        if j == 0:
            return jnp.where(ids == 0, x_first[q : q + 1], chunk_first[q])
        if j == count - 1:
            return jnp.where(ids == CHUNKS - 1, x_last[q : q + 1], chunk_last[q])
        here = pl.ds(j * CHUNKS, CHUNKS)
        return part_ref[q, here, :] + left_ref[here, :] * chunk_first[q] + right_ref[here, :] * chunk_last[q]

    return solution_at


def turn(count, from_ref, to_ref):
    for k in range(2):
        starts = [64 * t + c for c in range(4 * k, 4 * k + 4) for t in range(count // 8)]
        for i in range(2):
            tiles = [from_ref[i, pl.ds(start, 8, stride=CHUNKS), :] for start in starts]
            to_ref[k, i * LANES : (i + 1) * LANES, :] = jnp.concatenate(tiles, 0).T


def lane_half(h):
    return pl.ds(h * LANES, LANES)


def x_kernel(
    count, state_ref, viscous_ref, part_ref, left_ref, right_ref, inner_ref, pay_ref, aux_ref,
    held_ref, first_ref, last_ref, sems,
):
    copies = [
        pltpu.make_async_copy(viscous_ref.at[:, lane_half(h)], held_ref.at[h, FIELDS], sems.at[h, FIELDS])
        for h in range(2)
    ] + [
        pltpu.make_async_copy(state_ref.at[q, :, lane_half(h)], held_ref.at[h, q], sems.at[h, q])
        for h in range(2)
        for q in range(FIELDS)
    ]
    for copy in copies:
        copy.start()
    for copy in copies[:2]:
        copy.wait()

    def ready(h):
        for copy in copies[2 + FIELDS * h : 2 + FIELDS * (h + 1)]:
            copy.wait()

    def make_terms(h, j):
        density, mom_x, mom_y, mom_z, energy = (strided(held_ref.at[h, q], j, count) for q in range(FIELDS))
        inverse = 1.0 / density
        vel_x = (NEAR_SCALED * inverse) * mom_x
        kinetic = mom_x * mom_x + mom_y * mom_y + mom_z * mom_z
        press = GAMMA_MINUS * (energy - 0.5 * kinetic * inverse)
        here = pl.ds(j * CHUNKS, CHUNKS)
        aux_ref[h, 0, here, :] = (NEAR_SCALED * inverse) * mom_y
        aux_ref[h, 1, here, :] = press
        low, high, far = ONE_THIRD - vel_x, ONE_THIRD + vel_x, FAR_RATIO * vel_x

        def general(u, flux):
            third = ONE_THIRD * u
            return u, third - flux, third + flux, FAR_RATIO * flux

        def carried(u):
            return u, low * u, high * u, far * u

        return (
            general(density, NEAR_SCALED * mom_x),
            general(mom_x, mom_x * vel_x + NEAR_SCALED * press),
            carried(mom_y),
            carried(mom_z),
            general(energy, (energy + press) * vel_x),
        )

    def viscous_at(j):
        value = jnp.stack([strided(held_ref.at[h, FIELDS], j, count) for h in range(2)])
        aux_ref[:, 2, pl.ds(j * CHUNKS, CHUNKS), :] = value
        return value

    local_solve(
        ready, make_terms, viscous_at, count, part_ref, left_ref, right_ref, inner_ref, pay_ref, first_ref, last_ref
    )


def y_kernel(count, stages, me_ref, *refs):
    size, levels = stages[-1][1], len(stages) - 1
    pay_refs, own_refs, refs = refs[:size], refs[size : size + levels], refs[size + levels :]
    x_part_ref, x_left_ref, x_right_ref, x_inner_ref, aux_ref, *refs = refs
    part_ref, left_ref, right_ref, inner_ref, pay_ref, *refs = refs
    blocks_ref, table_ref, sol_ref, section_ref, turned_ref, first_ref, last_ref = refs
    ends = outer_solve(stages[-1], me_ref, pay_refs, own_refs, blocks_ref, table_ref)
    for i in range(3):
        turn(count, aux_ref.at[:, i], turned_ref.at[FIELDS + i])
    halves = [
        rebuild(
            ends[h], count, x_part_ref.at[h], x_left_ref.at[h], x_right_ref.at[h], x_inner_ref.at[h], sol_ref.at[h]
        )
        for h in range(2)
    ]
    for q in range(FIELDS):
        for h in range(2):
            for j in range(count):
                section_ref[q, h, pl.ds(j * CHUNKS, CHUNKS), :] = halves[h](q, j)
        turn(count, section_ref.at[q], turned_ref.at[q])

    def value(q, h, j):
        return strided(turned_ref.at[q, h], j, count)

    def make_terms(h, j):
        vel_y, press = value(FIELDS, h, j), value(FIELDS + 1, h, j)
        low, high, far = ONE_THIRD - vel_y, ONE_THIRD + vel_y, FAR_RATIO * vel_y

        def carried(u):
            return u, low * u, high * u, far * u

        def pressed(u, flux):
            return u, low * u - flux, high * u + flux, far * u + FAR_RATIO * flux

        return (
            carried(value(0, h, j)),
            carried(value(1, h, j)),
            pressed(value(2, h, j), NEAR_SCALED * press),
            carried(value(3, h, j)),
            pressed(value(4, h, j), press * vel_y),
        )

    def viscous_at(j):
        return jnp.stack([value(FIELDS + 2, h, j) for h in range(2)])

    local_solve(
        lambda h: None, make_terms, viscous_at, count,
        part_ref, left_ref, right_ref, inner_ref, pay_ref, first_ref, last_ref,
    )


def last_kernel(count, stages, me_ref, *refs):
    size, levels = stages[-1][1], len(stages) - 1
    pay_refs, own_refs, refs = refs[:size], refs[size : size + levels], refs[size + levels :]
    part_ref, left_ref, right_ref, inner_ref, new_ref, *refs = refs
    blocks_ref, table_ref, sol_ref, section_ref, turned_ref, sems = refs
    ends = outer_solve(stages[-1], me_ref, pay_refs, own_refs, blocks_ref, table_ref)
    halves = [
        rebuild(ends[h], count, part_ref.at[h], left_ref.at[h], right_ref.at[h], inner_ref.at[h], sol_ref.at[h])
        for h in range(2)
    ]
    copies = []
    for q in range(FIELDS):
        for h in range(2):
            for j in range(count):
                section_ref[q, h, pl.ds(j * CHUNKS, CHUNKS), :] = halves[h](q, j)
        turn(count, section_ref.at[q], turned_ref.at[q])
        for h in range(2):
            copies.append(
                pltpu.make_async_copy(turned_ref.at[q, h], new_ref.at[q, :, lane_half(h)], sems.at[q, h])
            )
            copies[-1].start()
    for copy in copies:
        copy.wait()


def shards(devices_x, devices_y, state, viscous):
    cells = state.shape[2]
    count = cells // CHUNKS
    float_of = lambda *shape: jax.ShapeDtypeStruct(shape, jnp.float32)
    memory = lambda *shape: pltpu.VMEM(shape, jnp.float32)
    params = pltpu.CompilerParams(vmem_limit_bytes=48 * 1024 * 1024)
    whole = pl.BlockSpec(memory_space=pltpu.VMEM)
    far = pl.BlockSpec(memory_space=pltpu.HBM)
    scalar = pl.BlockSpec(memory_space=pltpu.SMEM)
    solved_shapes = [
        float_of(2, FIELDS, cells, LANES), float_of(2, cells, LANES), float_of(2, cells, LANES),
        float_of(2, 128, LANES),
    ]
    pay_shape = (2, PAY_ROWS, LANES)
    *x_parts, x_pay, aux = pl.pallas_call(
        functools.partial(x_kernel, count),
        out_shape=solved_shapes + [float_of(*pay_shape), float_of(2, 3, cells, LANES)],
        in_specs=[far] * 2,
        out_specs=[whole] * 6,
        scratch_shapes=[
            memory(2, FIELDS + 1, cells, LANES), memory(2, 72, LANES), memory(2, 72, LANES),
            pltpu.SemaphoreType.DMA((2, FIELDS + 1)),
        ],
        compiler_params=params,
        name="x_lines",
    )(
        pltpu.with_memory_space_constraint(state.reshape(FIELDS, cells, cells), pltpu.HBM),
        pltpu.with_memory_space_constraint(viscous.reshape(cells, cells), pltpu.HBM),
    )
    me = (lax.axis_index("gx") * devices_y + lax.axis_index("gy")).astype(jnp.int32).reshape(1)
    def merge_scratch(stage):
        return [memory(stage[1], *pay_shape), memory(2, 32 * stage[1], LANES)]

    def gather(pay, axis, stages):
        owns = []
        for stage in stages:
            pays = [pay]
            for mask in stage[2]:
                pairs = [(i, i ^ mask) for i in range(lax.axis_size(axis))]
                pays.append(lax.ppermute(pay, axis, pairs))
            if stage is stages[-1]:
                return pays + owns[::-1]
            pay, own = pl.pallas_call(
                functools.partial(merge_kernel, stage),
                out_shape=[float_of(*pay_shape), float_of(2, 32, LANES)],
                in_specs=[scalar] + [whole] * stage[1],
                out_specs=[whole] * 2,
                scratch_shapes=merge_scratch(stage),
                compiler_params=params,
                name="merge_" + axis,
            )(me, *pays)
            owns.append(own)

    x_stages = ((devices_y, 2, (1,)), (2 * devices_y, 4, (2, 4, 6)), (8 * devices_y, 2, (14,)))
    y_stages = ((1, 4, (1, 2, 3)), (4, 4, (4, 8, 12)))
    x_ends = gather(x_pay, "gx", x_stages)
    *y_parts, y_pay = pl.pallas_call(
        functools.partial(y_kernel, count, x_stages),
        out_shape=solved_shapes + [float_of(*pay_shape)],
        in_specs=[scalar] + [whole] * (len(x_ends) + 5),
        out_specs=[whole] * 5,
        scratch_shapes=merge_scratch(x_stages[-1]) + [
            memory(2, 128, LANES), memory(FIELDS, 2, cells, LANES), memory(FIELDS + 3, 2, cells, LANES),
            memory(2, 72, LANES), memory(2, 72, LANES),
        ],
        compiler_params=params,
        name="y_lines",
    )(me, *x_ends, *x_parts, aux)
    y_ends = gather(y_pay, "gy", y_stages)
    new = pl.pallas_call(
        functools.partial(last_kernel, count, y_stages),
        out_shape=float_of(FIELDS, cells, cells),
        in_specs=[scalar] + [whole] * (len(y_ends) + 4),
        out_specs=far,
        scratch_shapes=merge_scratch(y_stages[-1]) + [
            memory(2, 128, LANES), memory(FIELDS, 2, cells, LANES), memory(FIELDS, 2, cells, LANES),
            pltpu.SemaphoreType.DMA((FIELDS, 2)),
        ],
        compiler_params=params,
        name="new_state",
    )(me, *y_ends, *y_parts)
    return new.reshape(state.shape)


def solution(mesh):
    placed = (P(None, None, "gx", "gy"), P(None, "gx", "gy"))
    return jax.shard_map(
        functools.partial(shards, mesh.shape["gx"], mesh.shape["gy"]),
        mesh=mesh, in_specs=placed, out_specs=P(None, None, "gx", "gy"), check_vma=False,
    )
```

```python
import functools
import jax
import jax.numpy as jnp
from jax import lax
from jax.experimental import pallas as pl
from jax.experimental.pallas import tpu as pltpu
from jax.sharding import PartitionSpec as P

STEP_RATIO = 0.25
ONE_THIRD = 1.0 / 3.0
NEAR_WEIGHT = 7.0 / 9.0
FAR_WEIGHT = 1.0 / 36.0
GAMMA_MINUS = 0.4
NEAR_SCALED = STEP_RATIO * NEAR_WEIGHT
FAR_RATIO = FAR_WEIGHT / NEAR_WEIGHT
FIELDS = 5
CHUNKS = 8
LANES = 128
PAY_ROWS = 40
ROW_RIGHT, ROW_HI, ROW_FLUX_RIGHT, ROW_LEFT, ROW_FLUX_LEFT, ROW_LO = 16, 21, 22, 27, 32, 37


def strided(ref, position, count):
    return ref[pl.ds(position, CHUNKS, stride=count), :]


def sublane_ids(shape):
    return lax.broadcasted_iota(jnp.int32, shape, len(shape) - 2)


def from_previous(value):
    return jnp.where(sublane_ids(value.shape) == 0, 0.0, pltpu.roll(value, 1, value.ndim - 2))


def from_next(value):
    return jnp.where(sublane_ids(value.shape) == CHUNKS - 1, 0.0, pltpu.roll(value, CHUNKS - 1, value.ndim - 2))


class Matrix:
    def __init__(self, viscous_at, count):
        self.viscous_at, self.count, self.known = viscous_at, count, {}

    def viscous(self, j):
        if j not in self.known:
            if j < 0:
                value = from_previous(self.viscous(j + self.count))
            elif j >= self.count:
                value = from_next(self.viscous(j - self.count))
            else:
                value = self.viscous_at(j)
            self.known[j] = value
        return self.known[j]

    def face(self, j):
        return 0.5 * (self.viscous(j - 1) + self.viscous(j))

    def coupling(self, j):
        return ONE_THIRD - self.face(j)

    def diagonal(self, j):
        return 1.0 + self.face(j) + self.face(j + 1)


class Rows:
    def __init__(self, ref):
        self.ref = ref

    def __getitem__(self, j):
        return self.ref[:, pl.ds(j * CHUNKS, CHUNKS), :]

    def __setitem__(self, j, value):
        self.ref[:, pl.ds(j * CHUNKS, CHUNKS), :] = value


def eliminate_matrix(matrix, inverse, tied, slope, left, right):
    final, middle = matrix.count - 1, matrix.count // 2
    pivots, slopes, reach = {}, {}, {}
    for k in range(1, middle):
        for j, before, outer, inner in ((k, k - 1, k, k + 1), (final - k, final - k + 1, final - k + 1, final - k)):
            pivot = matrix.diagonal(j)
            if k > 1:
                pivot = pivot - matrix.coupling(outer) * slopes[before]
            pivots[j] = 1.0 / pivot
            bound = matrix.coupling(outer) * pivots[j]
            slopes[j] = matrix.coupling(inner) * pivots[j]
            reach[j] = -bound if k == 1 else -bound * reach[before]
            inverse[j], tied[j], slope[j] = pivots[j], bound, slopes[j]
    low, high = middle - 1, middle
    meet = 1.0 / (1.0 - slopes[low] * slopes[high])
    inverse[0] = meet
    lefts, rights = {}, {}
    lefts[low], rights[low] = reach[low] * meet, -(slopes[low] * reach[high]) * meet
    lefts[high], rights[high] = -slopes[high] * lefts[low], reach[high] - slopes[high] * rights[low]
    for k in range(middle - 2, 0, -1):
        lefts[k], rights[k] = reach[k] - slopes[k] * lefts[k + 1], -slopes[k] * rights[k + 1]
        m = final - k
        lefts[m], rights[m] = -slopes[m] * lefts[m - 1], reach[m] - slopes[m] * rights[m - 1]
    for j in range(1, final):
        left[j], right[j] = lefts[j], rights[j]


def local_solve(ready, make_terms, matrix, factors, part_ref, inner_ref, pay_ref, first_ref, last_ref):
    count = matrix.count
    final, middle = count - 1, count // 2
    low, high = middle - 1, middle
    rows = lambda j: pl.ds(j * CHUNKS, CHUNKS)
    viscous, face, coupling, diagonal = matrix.viscous, matrix.face, matrix.coupling, matrix.diagonal
    inverse, tied, slope, all_left, all_right = factors
    meet = inverse[0]
    left, right = ({j: value[j] for j in (1, final - 1)} for value in (all_left, all_right))

    first = lambda value: value[..., 0:1, :]
    last = lambda value: value[..., CHUNKS - 1 : CHUNKS, :]
    up_first, low_last = coupling(1), coupling(final)
    fields = range(FIELDS)
    for h in range(2):
        ready(h)
        ends, carried = {}, None

        def take(j, sums):
            nonlocal carried
            if j == 0 or j == final:
                ends[j] = sums
                return
            if j == 1:
                carried = [s * inverse[j][h] for s in sums]
            elif j < middle:
                carried = [s * inverse[j][h] - tied[j][h] * f for s, f in zip(sums, carried)]
            for q in fields:
                part_ref[h, q, rows(j), :] = carried[q] if j < middle else sums[q]

        before, end = make_terms(h, final - 1), make_terms(h, final)
        for q in fields:
            pay_ref[h, ROW_RIGHT + q : ROW_RIGHT + q + 1, :] = last(end[q][2] + before[q][3])
            pay_ref[h, ROW_FLUX_RIGHT + q : ROW_FLUX_RIGHT + q + 1, :] = last(end[q][3])
        sums = {
            0: [from_previous(end[q][2] + before[q][3]) for q in fields],
            1: [from_previous(end[q][3]) for q in fields],
        }
        for j in range(count):
            terms = make_terms(h, j)
            if j == 0:
                zero = terms
            if j == 1:
                above_last = [from_next(zero[q][1] - terms[q][3]) for q in fields]
                above_before = [from_next(zero[q][3]) for q in fields]
                for q in fields:
                    to_left = first(zero[q][1] - terms[q][3])
                    pay_ref[h, ROW_LEFT + q : ROW_LEFT + q + 1, :] = to_left
                    pay_ref[h, ROW_FLUX_LEFT + q : ROW_FLUX_LEFT + q + 1, :] = -first(zero[q][3])
            if j >= 2:
                take(j - 2, [sums[j - 2][q] - terms[q][3] for q in fields])
                del sums[j - 2]
            if j >= 1:
                sums[j - 1] = [sums[j - 1][q] + terms[q][1] for q in fields]
            sums[j] = [sums[j][q] + terms[q][0] for q in fields]
            if j < final:
                if j == 0:
                    sums[1] = [sums[1][q] + terms[q][2] for q in fields]
                else:
                    sums[j + 1] = [sums[j + 1][q] + terms[q][2] for q in fields]
            if j < final - 1:
                sums[j + 2] = [terms[q][3] for q in fields]
        take(final - 1, [sums[final - 1][q] - above_before[q] for q in fields])
        take(final, [sums[final][q] + above_last[q] for q in fields])

        upper = None
        for j in range(final - 1, middle - 1, -1):
            values = [part_ref[h, q, rows(j), :] for q in fields]
            if upper is None:
                upper = [s * inverse[j][h] for s in values]
            else:
                upper = [s * inverse[j][h] - tied[j][h] * f for s, f in zip(values, upper)]
            if j > middle:
                for q in fields:
                    part_ref[h, q, rows(j), :] = upper[q]
        solved_low = [(a - slope[low][h] * b) * meet[h] for a, b in zip(carried, upper)]
        solved_high = [b - slope[high][h] * a for a, b in zip(solved_low, upper)]
        for q in fields:
            part_ref[h, q, rows(low), :] = solved_low[q]
            part_ref[h, q, rows(high), :] = solved_high[q]
        for k in range(middle - 2, 0, -1):
            solved_low = [part_ref[h, q, rows(k), :] - slope[k][h] * solved_low[q] for q in fields]
            m = final - k
            solved_high = [part_ref[h, q, rows(m), :] - slope[m][h] * solved_high[q] for q in fields]
            for q in fields:
                part_ref[h, q, rows(k), :] = solved_low[q]
                part_ref[h, q, rows(m), :] = solved_high[q]
        for q in fields:
            first_ref[h, pl.ds(q, CHUNKS, stride=8), :] = ends[0][q] - up_first[h] * solved_low[q]
            last_ref[h, pl.ds(q, CHUNKS, stride=8), :] = ends[final][q] - low_last[h] * solved_high[q]
            pay_ref[h, q : q + 1, :] = first(solved_low[q])
            pay_ref[h, 8 + q : 9 + q, :] = last(solved_high[q])
            first_ref[h, 64 + q : 65 + q, :] = first(ends[0][q])
            last_ref[h, 64 + q : 65 + q, :] = last(ends[final][q])
        zeros = jnp.zeros((CHUNKS, LANES), jnp.float32)
        ids = sublane_ids(zeros.shape)
        first_ref[h, pl.ds(5, CHUNKS, stride=8), :] = zeros
        first_ref[h, pl.ds(6, CHUNKS, stride=8), :] = jnp.where(ids == CHUNKS - 1, -up_first[h] * right[1][h], zeros)
        first_ref[h, pl.ds(7, CHUNKS, stride=8), :] = zeros
        last_ref[h, pl.ds(5, CHUNKS, stride=8), :] = jnp.where(ids == 0, -low_last[h] * left[final - 1][h], zeros)
        last_ref[h, pl.ds(6, CHUNKS, stride=8), :] = zeros
        last_ref[h, pl.ds(7, CHUNKS, stride=8), :] = zeros
        pay_ref[h, 5:6, :] = first(left[1][h])
        pay_ref[h, 6:8, :] = zeros[0:2]
        pay_ref[h, 13:14, :] = zeros[0:1]
        pay_ref[h, 14:15, :] = last(right[final - 1][h])
        pay_ref[h, 15:16, :] = zeros[0:1]

    def row(value, c):
        return value[:, c : c + 1, :]

    first_low, first_diag, first_up = coupling(0), diagonal(0) + up_first * left[1], up_first * right[1]
    last_low, last_diag = low_last * left[final - 1], diagonal(final) + low_last * right[final - 1]
    last_up = coupling(count)
    chain = []
    for c in range(CHUNKS):
        if c > 0:
            rhs = first_ref[:, 8 * c : 8 * c + 8, :]
            chain.append((row(first_low, c), row(first_diag, c), row(first_up, c), rhs))
        if c < CHUNKS - 1:
            rhs = last_ref[:, 8 * c : 8 * c + 8, :]
            chain.append((row(last_low, c), row(last_diag, c), row(last_up, c), rhs))
    solved = solve_chain(chain)
    inner_ref[:, 0:8, :] = jnp.zeros_like(solved[0])
    inner_ref[:, 120:128, :] = jnp.zeros_like(solved[0])
    for m, value in enumerate(solved):
        inner_ref[:, 8 * m + 8 : 8 * m + 16, :] = value

    eight = sublane_ids((2, 8, LANES))
    second = pay_ref[:, 0:8, :] + row(right[1], 0) * solved[0]
    pay_ref[:, 0:8, :] = jnp.where(eight < FIELDS, first_ref[:, 64:72, :] - row(up_first, 0) * second, second)
    second = pay_ref[:, 8:16, :] + row(left[final - 1], CHUNKS - 1) * solved[-1]
    pay_ref[:, 8:16, :] = jnp.where(
        eight < FIELDS, last_ref[:, 64:72, :] - row(low_last, CHUNKS - 1) * second, second
    )
    pay_ref[:, 7:8, :] = first(viscous(0))
    pay_ref[:, 15:16, :] = last(viscous(final))
    pay_ref[:, ROW_HI : ROW_HI + 1, :] = first(face(1))
    pay_ref[:, ROW_LO : ROW_LO + 1, :] = last(face(final))
    pay_ref[:, 38:40, :] = jnp.zeros((2, 2, LANES), jnp.float32)


def solve_chain(chain):
    size, middle = len(chain), len(chain) // 2
    slope, value = [None] * size, [None] * size
    for k in range(middle):
        for m, before in ((k, k - 1), (size - 1 - k, size - k)):
            low, diag, up, rhs = chain[m]
            outer, inner = (low, up) if m < middle else (up, low)
            if k > 0:
                diag = diag - outer * slope[before]
                rhs = rhs - outer * value[before]
            inverse = 1.0 / diag
            value[m] = rhs * inverse
            slope[m] = inner * inverse
    a, b = middle - 1, middle
    value[a] = (value[a] - slope[a] * value[b]) * (1.0 / (1.0 - slope[a] * slope[b]))
    value[b] = value[b] - slope[b] * value[a]
    for k in range(middle - 2, -1, -1):
        value[k] = value[k] - slope[k] * value[k + 1]
        m = size - 1 - k
        value[m] = value[m] - slope[m] * value[m - 1]
    return value


def join(blocks, at_ends):
    count = len(blocks)
    one = lambda b, row: blocks[b](row, 1)
    face = lambda b: 0.5 * (one(b, 15) + one(b + 1, 7))
    chain, deltas, scales = [], [], []
    for b in range(count):
        rhs_first, rhs_last = blocks[b](0, 8), blocks[b](8, 8)
        second = before = None
        if b > 0:
            second = blocks[b - 1](ROW_FLUX_RIGHT, 8)
            rhs_first = rhs_first + blocks[b - 1](ROW_RIGHT, 8) + one(b, 5) * second
            rhs_last = rhs_last + one(b, 6) * second
        if b < count - 1:
            before = blocks[b + 1](ROW_FLUX_LEFT, 8)
            rhs_first = rhs_first + one(b, 13) * before
            rhs_last = rhs_last + blocks[b + 1](ROW_LEFT, 8) + one(b, 14) * before
        up, low = ONE_THIRD - one(b, ROW_HI), ONE_THIRD - one(b, ROW_LO)
        lo_first = face(b - 1) if b > 0 else 0.5 * one(b, 7)
        hi_last = face(b) if b < count - 1 else 0.5 * one(b, 15)
        zero = jnp.zeros_like(up)
        outer_low = ONE_THIRD - lo_first if b > 0 else zero
        outer_up = ONE_THIRD - hi_last if b < count - 1 else zero
        chain.append((outer_low, (1.0 + lo_first + one(b, ROW_HI)) + up * one(b, 5), up * one(b, 6), rhs_first))
        chain.append((low * one(b, 13), (1.0 + one(b, ROW_LO) + hi_last) + low * one(b, 14), outer_up, rhs_last))
        deltas.append((second, before))
        scales.append((up, low))
    return chain if at_ends else chain[1:-1], chain[0], chain[-1], deltas, scales


def ordered(stage, place, pay_refs, blocks_ref):
    for k, pay_ref in zip((0,) + tuple(stage[2]), pay_refs):
        blocks_ref[jnp.bitwise_xor(place, k)] = pay_ref[...]
    return [lambda row, size, b=b: blocks_ref[b, :, row : row + size, :] for b in range(len(pay_refs))]


def place_in(stage, me_ref):
    first, size, _ = stage
    return lax.rem(me_ref[0] // first, size)


def merge_kernel(stage, me_ref, *refs):
    size = stage[1]
    pay_refs, (merged_ref, own_ref, blocks_ref, table_ref) = refs[:size], refs[size:]
    place = place_in(stage, me_ref)
    blocks = ordered(stage, place, pay_refs, blocks_ref)
    chain, first, last, deltas, scales = join(blocks, False)
    eight = sublane_ids((2, 8, LANES))
    is_field = eight < FIELDS
    rhs = [jnp.where(is_field, value, 0.0) for _, _, _, value in chain]
    rhs[0] = jnp.where(eight == 5, -chain[0][0], rhs[0])
    rhs[-1] = jnp.where(eight == 6, -chain[-1][2], rhs[-1])
    inner = solve_chain([(low, diag, up, value) for (low, diag, up, _), value in zip(chain, rhs)])

    merged_ref[:, 0:8, :] = first[3] - first[2] * inner[0]
    merged_ref[:, 8:16, :] = last[3] - last[0] * inner[-1]
    merged_ref[:, 5:6, :] = blocks[0](5, 1) + blocks[0](6, 1) * inner[0][:, 5:6, :]
    merged_ref[:, 6:7, :] = blocks[0](6, 1) * inner[0][:, 6:7, :]
    merged_ref[:, 7:8, :] = blocks[0](7, 1)
    merged_ref[:, 13:14, :] = blocks[-1](13, 1) * inner[-1][:, 5:6, :]
    merged_ref[:, 14:15, :] = blocks[-1](14, 1) + blocks[-1](13, 1) * inner[-1][:, 6:7, :]
    merged_ref[:, 15:16, :] = blocks[-1](15, 1)
    for row, rows, block in (
        (ROW_RIGHT, 5, -1), (ROW_HI, 1, 0), (ROW_FLUX_RIGHT, 5, -1), (ROW_LEFT, 10, 0), (ROW_LO, 1, -1)
    ):
        merged_ref[:, row : row + rows, :] = blocks[block](row, rows)
    merged_ref[:, 38:40, :] = jnp.zeros((2, 2, LANES), jnp.float32)

    for b in range(size):
        zero = jnp.zeros((2, 8, LANES), jnp.float32)
        own_first = jnp.where((eight == 5) | (eight == 7), 1.0, zero) if b == 0 else inner[2 * b - 1]
        own_last = jnp.where((eight == 6) | (eight == 7), 1.0, zero) if b == size - 1 else inner[2 * b]
        second, before = deltas[b]
        second = zero if second is None else jnp.where(is_field, second / scales[b][0], 0.0)
        before = zero if before is None else jnp.where(is_field, before / scales[b][1], 0.0)
        for i, value in enumerate((own_first, own_last, second, before)):
            table_ref[:, b * 32 + 8 * i : b * 32 + 8 * i + 8, :] = value
    own_ref[...] = table_ref[:, pl.ds(pl.multiple_of(place * 32, 32), 32), :]


def outer_solve(stage, me_ref, pay_refs, own_refs, blocks_ref, table_ref):
    place = place_in(stage, me_ref)
    chain, _, _, deltas, scales = join(ordered(stage, place, pay_refs, blocks_ref), True)
    solved = solve_chain(chain)
    for b in range(stage[1]):
        x_first, x_last = solved[2 * b], solved[2 * b + 1]
        second, before = deltas[b]
        seen_first = x_first if second is None else x_first - second / scales[b][0]
        seen_last = x_last if before is None else x_last - before / scales[b][1]
        for i, value in enumerate((x_first, x_last, seen_first, seen_last)):
            table_ref[:, b * 32 + 8 * i : b * 32 + 8 * i + 8, :] = value
    mine = table_ref[:, pl.ds(pl.multiple_of(place * 32, 32), 32), :]
    ends = [mine[:, 8 * i : 8 * i + 8] for i in range(4)]
    for own_ref in own_refs:
        x_first, x_last, seen_first, seen_last = ends
        own_first, own_last, second, before = (own_ref[:, 8 * i : 8 * i + 8, :] for i in range(4))
        first = own_first + own_first[:, 5:6] * seen_first + own_first[:, 6:7] * seen_last
        last = own_last + own_last[:, 5:6] * seen_first + own_last[:, 6:7] * seen_last
        ends = [
            first + own_first[:, 7:8] * (x_first - seen_first),
            last + own_last[:, 7:8] * (x_last - seen_last),
            first - second,
            last - before,
        ]
    return [[value[h] for value in ends] for h in range(2)]


def rebuild(ends, count, part_ref, left_ref, right_ref, inner_ref, sol_ref):
    x_first, x_last, seen_first, seen_last = ends
    for m in range(16):
        if m == 0:
            value = seen_first
        elif m == 15:
            value = seen_last
        else:
            inner = inner_ref[8 * m : 8 * m + 8, :]
            value = inner + inner[5:6] * seen_first + inner[6:7] * seen_last
        sol_ref[8 * m : 8 * m + 8, :] = value
    chunk_first = [sol_ref[pl.ds(q, CHUNKS, stride=16), :] for q in range(FIELDS)]
    chunk_last = [sol_ref[pl.ds(8 + q, CHUNKS, stride=16), :] for q in range(FIELDS)]
    ids = sublane_ids(chunk_first[0].shape)

    def solution_at(q, j):
        if j == 0:
            return jnp.where(ids == 0, x_first[q : q + 1], chunk_first[q])
        if j == count - 1:
            return jnp.where(ids == CHUNKS - 1, x_last[q : q + 1], chunk_last[q])
        here = pl.ds(j * CHUNKS, CHUNKS)
        return part_ref[q, here, :] + left_ref[here, :] * chunk_first[q] + right_ref[here, :] * chunk_last[q]

    return solution_at


def turn(count, from_ref, to_ref):
    for k in range(2):
        starts = [64 * t + c for c in range(4 * k, 4 * k + 4) for t in range(count // 8)]
        for i in range(2):
            tiles = [from_ref[i, pl.ds(start, 8, stride=CHUNKS), :] for start in starts]
            to_ref[k, i * LANES : (i + 1) * LANES, :] = jnp.concatenate(tiles, 0).T


def lane_half(h):
    return pl.ds(h * LANES, LANES)


def x_kernel(
    count, state_ref, viscous_ref, part_ref, left_ref, right_ref, inner_ref, pay_ref, aux_ref,
    held_ref, first_ref, last_ref, sems,
):
    copies = [
        pltpu.make_async_copy(viscous_ref.at[:, lane_half(h)], held_ref.at[h, FIELDS], sems.at[h, FIELDS])
        for h in range(2)
    ] + [
        pltpu.make_async_copy(state_ref.at[q, :, lane_half(h)], held_ref.at[h, q], sems.at[h, q])
        for h in range(2)
        for q in range(FIELDS)
    ]
    for copy in copies:
        copy.start()
    for copy in copies[:2]:
        copy.wait()

    def ready(h):
        for copy in copies[2 + FIELDS * h : 2 + FIELDS * (h + 1)]:
            copy.wait()

    def make_terms(h, j):
        density, mom_x, mom_y, mom_z, energy = (strided(held_ref.at[h, q], j, count) for q in range(FIELDS))
        inverse = 1.0 / density
        vel_x = (NEAR_SCALED * inverse) * mom_x
        kinetic = mom_x * mom_x + mom_y * mom_y + mom_z * mom_z
        press = GAMMA_MINUS * (energy - 0.5 * kinetic * inverse)
        here = pl.ds(j * CHUNKS, CHUNKS)
        aux_ref[h, 0, here, :] = (NEAR_SCALED * inverse) * mom_y
        aux_ref[h, 1, here, :] = press
        low, high, far = ONE_THIRD - vel_x, ONE_THIRD + vel_x, FAR_RATIO * vel_x

        def general(u, flux):
            third = ONE_THIRD * u
            return u, third - flux, third + flux, FAR_RATIO * flux

        def carried(u):
            return u, low * u, high * u, far * u

        return (
            general(density, NEAR_SCALED * mom_x),
            general(mom_x, mom_x * vel_x + NEAR_SCALED * press),
            carried(mom_y),
            carried(mom_z),
            general(energy, (energy + press) * vel_x),
        )

    def viscous_at(j):
        value = jnp.stack([strided(held_ref.at[h, FIELDS], j, count) for h in range(2)])
        aux_ref[:, 2, pl.ds(j * CHUNKS, CHUNKS), :] = value
        return value

    matrix, factors = Matrix(viscous_at, count), ({}, {}, {}, Rows(left_ref), Rows(right_ref))
    eliminate_matrix(matrix, *factors)
    local_solve(ready, make_terms, matrix, factors, part_ref, inner_ref, pay_ref, first_ref, last_ref)


def y_matrix_kernel(count, aux_ref, turned_ref, inverse_ref, tied_ref, slope_ref, left_ref, right_ref):
    for i in range(3):
        turn(count, aux_ref.at[:, i], turned_ref.at[i])
    matrix = Matrix(lambda j: jnp.stack([strided(turned_ref.at[2, h], j, count) for h in range(2)]), count)
    eliminate_matrix(matrix, *map(Rows, (inverse_ref, tied_ref, slope_ref, left_ref, right_ref)))
    inverse_ref[:, (count - 1) * CHUNKS :, :] = jnp.zeros((2, CHUNKS, LANES), jnp.float32)


def y_kernel(count, stages, me_ref, *refs):
    size, levels = stages[-1][1], len(stages) - 1
    pay_refs, own_refs, refs = refs[:size], refs[size : size + levels], refs[size + levels :]
    x_part_ref, x_left_ref, x_right_ref, x_inner_ref, aux_ref, *refs = refs
    inverse_ref, tied_ref, slope_ref, left_ref, right_ref, part_ref, inner_ref, pay_ref, *refs = refs
    blocks_ref, table_ref, sol_ref, section_ref, turned_ref, first_ref, last_ref = refs
    ends = outer_solve(stages[-1], me_ref, pay_refs, own_refs, blocks_ref, table_ref)
    halves = [
        rebuild(
            ends[h], count, x_part_ref.at[h], x_left_ref.at[h], x_right_ref.at[h], x_inner_ref.at[h], sol_ref.at[h]
        )
        for h in range(2)
    ]
    for q in range(FIELDS):
        for h in range(2):
            for j in range(count):
                section_ref[q, h, pl.ds(j * CHUNKS, CHUNKS), :] = halves[h](q, j)
        turn(count, section_ref.at[q], turned_ref.at[q])

    def value(q, h, j):
        return strided(turned_ref.at[q, h], j, count)

    def make_terms(h, j):
        vel_y, press = strided(aux_ref.at[0, h], j, count), strided(aux_ref.at[1, h], j, count)
        low, high, far = ONE_THIRD - vel_y, ONE_THIRD + vel_y, FAR_RATIO * vel_y

        def carried(u):
            return u, low * u, high * u, far * u

        def pressed(u, flux):
            return u, low * u - flux, high * u + flux, far * u + FAR_RATIO * flux

        return (
            carried(value(0, h, j)),
            carried(value(1, h, j)),
            pressed(value(2, h, j), NEAR_SCALED * press),
            carried(value(3, h, j)),
            pressed(value(4, h, j), press * vel_y),
        )

    def viscous_at(j):
        return jnp.stack([strided(aux_ref.at[2, h], j, count) for h in range(2)])

    factors = tuple(map(Rows, (inverse_ref, tied_ref, slope_ref, left_ref, right_ref)))
    local_solve(
        lambda h: None, make_terms, Matrix(viscous_at, count), factors,
        part_ref, inner_ref, pay_ref, first_ref, last_ref,
    )


def last_kernel(count, stages, me_ref, *refs):
    size, levels = stages[-1][1], len(stages) - 1
    pay_refs, own_refs, refs = refs[:size], refs[size : size + levels], refs[size + levels :]
    part_ref, left_ref, right_ref, inner_ref, new_ref, *refs = refs
    blocks_ref, table_ref, sol_ref, section_ref, turned_ref, sems = refs
    ends = outer_solve(stages[-1], me_ref, pay_refs, own_refs, blocks_ref, table_ref)
    halves = [
        rebuild(ends[h], count, part_ref.at[h], left_ref.at[h], right_ref.at[h], inner_ref.at[h], sol_ref.at[h])
        for h in range(2)
    ]
    copies = []
    for q in range(FIELDS):
        for h in range(2):
            for j in range(count):
                section_ref[q, h, pl.ds(j * CHUNKS, CHUNKS), :] = halves[h](q, j)
        turn(count, section_ref.at[q], turned_ref.at[q])
        for h in range(2):
            copies.append(
                pltpu.make_async_copy(turned_ref.at[q, h], new_ref.at[q, :, lane_half(h)], sems.at[q, h])
            )
            copies[-1].start()
    for copy in copies:
        copy.wait()


def shards(devices_x, devices_y, state, viscous):
    cells = state.shape[2]
    count = cells // CHUNKS
    float_of = lambda *shape: jax.ShapeDtypeStruct(shape, jnp.float32)
    memory = lambda *shape: pltpu.VMEM(shape, jnp.float32)
    params = pltpu.CompilerParams(vmem_limit_bytes=48 * 1024 * 1024)
    whole = pl.BlockSpec(memory_space=pltpu.VMEM)
    far = pl.BlockSpec(memory_space=pltpu.HBM)
    scalar = pl.BlockSpec(memory_space=pltpu.SMEM)
    solved_shapes = [
        float_of(2, FIELDS, cells, LANES), float_of(2, cells, LANES), float_of(2, cells, LANES),
        float_of(2, 128, LANES),
    ]
    pay_shape = (2, PAY_ROWS, LANES)
    *x_parts, x_pay, aux = pl.pallas_call(
        functools.partial(x_kernel, count),
        out_shape=solved_shapes + [float_of(*pay_shape), float_of(2, 3, cells, LANES)],
        in_specs=[far] * 2,
        out_specs=[whole] * 6,
        scratch_shapes=[
            memory(2, FIELDS + 1, cells, LANES), memory(2, 72, LANES), memory(2, 72, LANES),
            pltpu.SemaphoreType.DMA((2, FIELDS + 1)),
        ],
        compiler_params=params,
        name="x_lines",
    )(
        pltpu.with_memory_space_constraint(state.reshape(FIELDS, cells, cells), pltpu.HBM),
        pltpu.with_memory_space_constraint(viscous.reshape(cells, cells), pltpu.HBM),
    )
    me = (lax.axis_index("gx") * devices_y + lax.axis_index("gy")).astype(jnp.int32).reshape(1)
    def merge_scratch(stage):
        return [memory(stage[1], *pay_shape), memory(2, 32 * stage[1], LANES)]

    def gather(pay, axis, stages):
        owns = []
        for stage in stages:
            pays = [pay]
            for mask in stage[2].values():
                pairs = [(i, i ^ mask) for i in range(lax.axis_size(axis))]
                pays.append(lax.ppermute(pay, axis, pairs))
            if stage is stages[-1]:
                return pays + owns[::-1]
            pay, own = pl.pallas_call(
                functools.partial(merge_kernel, stage),
                out_shape=[float_of(*pay_shape), float_of(2, 32, LANES)],
                in_specs=[scalar] + [whole] * stage[1],
                out_specs=[whole] * 2,
                scratch_shapes=merge_scratch(stage),
                compiler_params=params,
                name="merge_" + axis,
            )(me, *pays)
            owns.append(own)

    x_stages = (
        (devices_y, 2, {1: 1}),
        (2 * devices_y, 4, {1: 2, 2: 4, 3: 6}),
        (8 * devices_y, 2, {1: 12}),
    )
    y_stages = ((1, 4, {1: 1, 3: 3, 2: 2}), (4, 4, {1: 4, 3: 12, 2: 8}))
    x_ends = gather(x_pay, "gx", x_stages)
    plane = float_of(2, cells, LANES)
    y_aux, *y_factors = pl.pallas_call(
        functools.partial(y_matrix_kernel, count),
        out_shape=[float_of(3, 2, cells, LANES)] + [plane] * 5,
        in_specs=[whole],
        out_specs=[whole] * 6,
        compiler_params=params,
        cost_estimate=pl.CostEstimate(flops=4000000, bytes_accessed=2000000, transcendentals=0),
        name="y_matrix",
    )(aux)
    y_part, y_inner, y_pay = pl.pallas_call(
        functools.partial(y_kernel, count, x_stages),
        out_shape=[solved_shapes[0], solved_shapes[3], float_of(*pay_shape)],
        in_specs=[scalar] + [whole] * (len(x_ends) + 10),
        out_specs=[whole] * 3,
        scratch_shapes=merge_scratch(x_stages[-1]) + [
            memory(2, 128, LANES), memory(FIELDS, 2, cells, LANES), memory(FIELDS, 2, cells, LANES),
            memory(2, 72, LANES), memory(2, 72, LANES),
        ],
        compiler_params=params,
        name="y_lines",
    )(me, *x_ends, *x_parts, y_aux, *y_factors)
    y_ends = gather(y_pay, "gy", y_stages)
    new = pl.pallas_call(
        functools.partial(last_kernel, count, y_stages),
        out_shape=float_of(FIELDS, cells, cells),
        in_specs=[scalar] + [whole] * (len(y_ends) + 4),
        out_specs=far,
        scratch_shapes=merge_scratch(y_stages[-1]) + [
            memory(2, 128, LANES), memory(FIELDS, 2, cells, LANES), memory(FIELDS, 2, cells, LANES),
            pltpu.SemaphoreType.DMA((FIELDS, 2)),
        ],
        compiler_params=params,
        name="new_state",
    )(me, *y_ends, y_part, *y_factors[3:], y_inner)
    return new.reshape(state.shape)


def solution(mesh):
    placed = (P(None, None, "gx", "gy"), P(None, "gx", "gy"))
    return jax.shard_map(
        functools.partial(shards, mesh.shape["gx"], mesh.shape["gy"]),
        mesh=mesh, in_specs=placed, out_specs=P(None, None, "gx", "gy"), check_vma=False,
    )
```

```python
import functools
import jax
import jax.numpy as jnp
from jax import lax
from jax.experimental import pallas as pl
from jax.experimental.pallas import tpu as pltpu
from jax.sharding import PartitionSpec as P

STEP_RATIO = 0.25
ONE_THIRD = 1.0 / 3.0
NEAR_WEIGHT = 7.0 / 9.0
FAR_WEIGHT = 1.0 / 36.0
GAMMA_MINUS = 0.4
NEAR_SCALED = STEP_RATIO * NEAR_WEIGHT
FAR_RATIO = FAR_WEIGHT / NEAR_WEIGHT
FIELDS = 5
CHUNKS = 8
LANES = 128
PAY_ROWS = 40
ROW_RIGHT, ROW_HI, ROW_FLUX_RIGHT, ROW_LEFT, ROW_FLUX_LEFT, ROW_LO = 16, 21, 22, 27, 32, 37


def strided(ref, position, count):
    return ref[pl.ds(position, CHUNKS, stride=count), :]


def sublane_ids(shape):
    return lax.broadcasted_iota(jnp.int32, shape, len(shape) - 2)


def from_previous(value):
    return jnp.where(sublane_ids(value.shape) == 0, 0.0, pltpu.roll(value, 1, value.ndim - 2))


def from_next(value):
    return jnp.where(sublane_ids(value.shape) == CHUNKS - 1, 0.0, pltpu.roll(value, CHUNKS - 1, value.ndim - 2))


class Matrix:
    def __init__(self, viscous_at, count):
        self.viscous_at, self.count, self.known = viscous_at, count, {}

    def viscous(self, j):
        if j not in self.known:
            if j < 0:
                value = from_previous(self.viscous(j + self.count))
            elif j >= self.count:
                value = from_next(self.viscous(j - self.count))
            else:
                value = self.viscous_at(j)
            self.known[j] = value
        return self.known[j]

    def face(self, j):
        return 0.5 * (self.viscous(j - 1) + self.viscous(j))

    def coupling(self, j):
        return ONE_THIRD - self.face(j)

    def diagonal(self, j):
        return 1.0 + self.face(j) + self.face(j + 1)


class Rows:
    def __init__(self, ref):
        self.ref = ref

    def __getitem__(self, j):
        return self.ref[:, pl.ds(j * CHUNKS, CHUNKS), :]

    def __setitem__(self, j, value):
        self.ref[:, pl.ds(j * CHUNKS, CHUNKS), :] = value


def eliminate_matrix(matrix, inverse, tied, slope, left, right):
    final, middle = matrix.count - 1, matrix.count // 2
    pivots, slopes, reach = {}, {}, {}
    for k in range(1, middle):
        for j, before, outer, inner in ((k, k - 1, k, k + 1), (final - k, final - k + 1, final - k + 1, final - k)):
            pivot = matrix.diagonal(j)
            if k > 1:
                pivot = pivot - matrix.coupling(outer) * slopes[before]
            pivots[j] = 1.0 / pivot
            bound = matrix.coupling(outer) * pivots[j]
            slopes[j] = matrix.coupling(inner) * pivots[j]
            reach[j] = -bound if k == 1 else -bound * reach[before]
            inverse[j], tied[j], slope[j] = pivots[j], bound, slopes[j]
    low, high = middle - 1, middle
    meet = 1.0 / (1.0 - slopes[low] * slopes[high])
    inverse[0] = meet
    lefts, rights = {}, {}
    lefts[low], rights[low] = reach[low] * meet, -(slopes[low] * reach[high]) * meet
    lefts[high], rights[high] = -slopes[high] * lefts[low], reach[high] - slopes[high] * rights[low]
    for k in range(middle - 2, 0, -1):
        lefts[k], rights[k] = reach[k] - slopes[k] * lefts[k + 1], -slopes[k] * rights[k + 1]
        m = final - k
        lefts[m], rights[m] = -slopes[m] * lefts[m - 1], reach[m] - slopes[m] * rights[m - 1]
    for j in range(1, final):
        left[j], right[j] = lefts[j], rights[j]


def local_solve(ready, make_terms, matrix, factors, part_ref, inner_ref, pay_ref, first_ref, last_ref):
    count = matrix.count
    final, middle = count - 1, count // 2
    low, high = middle - 1, middle
    rows = lambda j: pl.ds(j * CHUNKS, CHUNKS)
    viscous, face, coupling, diagonal = matrix.viscous, matrix.face, matrix.coupling, matrix.diagonal
    inverse, tied, slope, all_left, all_right = factors
    meet = inverse[0]
    left, right = ({j: value[j] for j in (1, final - 1)} for value in (all_left, all_right))

    first = lambda value: value[..., 0:1, :]
    last = lambda value: value[..., CHUNKS - 1 : CHUNKS, :]
    up_first, low_last = coupling(1), coupling(final)
    fields = range(FIELDS)
    for h in range(2):
        ready(h)
        ends, carried = {}, None

        def take(j, sums):
            nonlocal carried
            if j == 0 or j == final:
                ends[j] = sums
                return
            if j == 1:
                carried = [s * inverse[j][h] for s in sums]
            elif j < middle:
                carried = [s * inverse[j][h] - tied[j][h] * f for s, f in zip(sums, carried)]
            for q in fields:
                part_ref[h, q, rows(j), :] = carried[q] if j < middle else sums[q]

        before, end = make_terms(h, final - 1), make_terms(h, final)
        for q in fields:
            pay_ref[h, ROW_RIGHT + q : ROW_RIGHT + q + 1, :] = last(end[q][2] + before[q][3])
            pay_ref[h, ROW_FLUX_RIGHT + q : ROW_FLUX_RIGHT + q + 1, :] = last(end[q][3])
        sums = {
            0: [from_previous(end[q][2] + before[q][3]) for q in fields],
            1: [from_previous(end[q][3]) for q in fields],
        }
        for j in range(count):
            terms = {final - 1: before, final: end}.get(j) or make_terms(h, j)
            if j == 0:
                zero = terms
            if j == 1:
                above_last = [from_next(zero[q][1] - terms[q][3]) for q in fields]
                above_before = [from_next(zero[q][3]) for q in fields]
                for q in fields:
                    to_left = first(zero[q][1] - terms[q][3])
                    pay_ref[h, ROW_LEFT + q : ROW_LEFT + q + 1, :] = to_left
                    pay_ref[h, ROW_FLUX_LEFT + q : ROW_FLUX_LEFT + q + 1, :] = -first(zero[q][3])
            if j >= 2:
                take(j - 2, [sums[j - 2][q] - terms[q][3] for q in fields])
                del sums[j - 2]
            if j >= 1:
                sums[j - 1] = [sums[j - 1][q] + terms[q][1] for q in fields]
            sums[j] = [sums[j][q] + terms[q][0] for q in fields]
            if j < final:
                if j == 0:
                    sums[1] = [sums[1][q] + terms[q][2] for q in fields]
                else:
                    sums[j + 1] = [sums[j + 1][q] + terms[q][2] for q in fields]
            if j < final - 1:
                sums[j + 2] = [terms[q][3] for q in fields]
        take(final - 1, [sums[final - 1][q] - above_before[q] for q in fields])
        take(final, [sums[final][q] + above_last[q] for q in fields])

        upper = None
        for j in range(final - 1, middle - 1, -1):
            values = [part_ref[h, q, rows(j), :] for q in fields]
            if upper is None:
                upper = [s * inverse[j][h] for s in values]
            else:
                upper = [s * inverse[j][h] - tied[j][h] * f for s, f in zip(values, upper)]
            if j > middle:
                for q in fields:
                    part_ref[h, q, rows(j), :] = upper[q]
        solved_low = [(a - slope[low][h] * b) * meet[h] for a, b in zip(carried, upper)]
        solved_high = [b - slope[high][h] * a for a, b in zip(solved_low, upper)]
        for q in fields:
            part_ref[h, q, rows(low), :] = solved_low[q]
            part_ref[h, q, rows(high), :] = solved_high[q]
        for k in range(middle - 2, 0, -1):
            solved_low = [part_ref[h, q, rows(k), :] - slope[k][h] * solved_low[q] for q in fields]
            m = final - k
            solved_high = [part_ref[h, q, rows(m), :] - slope[m][h] * solved_high[q] for q in fields]
            for q in fields:
                part_ref[h, q, rows(k), :] = solved_low[q]
                part_ref[h, q, rows(m), :] = solved_high[q]
        for q in fields:
            first_ref[h, pl.ds(q, CHUNKS, stride=8), :] = ends[0][q] - up_first[h] * solved_low[q]
            last_ref[h, pl.ds(q, CHUNKS, stride=8), :] = ends[final][q] - low_last[h] * solved_high[q]
            pay_ref[h, q : q + 1, :] = first(solved_low[q])
            pay_ref[h, 8 + q : 9 + q, :] = last(solved_high[q])
            first_ref[h, 64 + q : 65 + q, :] = first(ends[0][q])
            last_ref[h, 64 + q : 65 + q, :] = last(ends[final][q])
        zeros = jnp.zeros((CHUNKS, LANES), jnp.float32)
        ids = sublane_ids(zeros.shape)
        first_ref[h, pl.ds(5, CHUNKS, stride=8), :] = zeros
        first_ref[h, pl.ds(6, CHUNKS, stride=8), :] = jnp.where(ids == CHUNKS - 1, -up_first[h] * right[1][h], zeros)
        first_ref[h, pl.ds(7, CHUNKS, stride=8), :] = zeros
        last_ref[h, pl.ds(5, CHUNKS, stride=8), :] = jnp.where(ids == 0, -low_last[h] * left[final - 1][h], zeros)
        last_ref[h, pl.ds(6, CHUNKS, stride=8), :] = zeros
        last_ref[h, pl.ds(7, CHUNKS, stride=8), :] = zeros
        pay_ref[h, 5:6, :] = first(left[1][h])
        pay_ref[h, 6:8, :] = zeros[0:2]
        pay_ref[h, 13:14, :] = zeros[0:1]
        pay_ref[h, 14:15, :] = last(right[final - 1][h])
        pay_ref[h, 15:16, :] = zeros[0:1]

    def row(value, c):
        return value[:, c : c + 1, :]

    first_low, first_diag, first_up = coupling(0), diagonal(0) + up_first * left[1], up_first * right[1]
    last_low, last_diag = low_last * left[final - 1], diagonal(final) + low_last * right[final - 1]
    last_up = coupling(count)
    chain = []
    for c in range(CHUNKS):
        if c > 0:
            rhs = first_ref[:, 8 * c : 8 * c + 8, :]
            chain.append((row(first_low, c), row(first_diag, c), row(first_up, c), rhs))
        if c < CHUNKS - 1:
            rhs = last_ref[:, 8 * c : 8 * c + 8, :]
            chain.append((row(last_low, c), row(last_diag, c), row(last_up, c), rhs))
    solved = solve_chain(chain)
    inner_ref[:, 0:8, :] = jnp.zeros_like(solved[0])
    inner_ref[:, 120:128, :] = jnp.zeros_like(solved[0])
    for m, value in enumerate(solved):
        inner_ref[:, 8 * m + 8 : 8 * m + 16, :] = value

    eight = sublane_ids((2, 8, LANES))
    second = pay_ref[:, 0:8, :] + row(right[1], 0) * solved[0]
    pay_ref[:, 0:8, :] = jnp.where(eight < FIELDS, first_ref[:, 64:72, :] - row(up_first, 0) * second, second)
    second = pay_ref[:, 8:16, :] + row(left[final - 1], CHUNKS - 1) * solved[-1]
    pay_ref[:, 8:16, :] = jnp.where(
        eight < FIELDS, last_ref[:, 64:72, :] - row(low_last, CHUNKS - 1) * second, second
    )
    pay_ref[:, 7:8, :] = first(viscous(0))
    pay_ref[:, 15:16, :] = last(viscous(final))
    pay_ref[:, ROW_HI : ROW_HI + 1, :] = first(face(1))
    pay_ref[:, ROW_LO : ROW_LO + 1, :] = last(face(final))
    pay_ref[:, 38:40, :] = jnp.zeros((2, 2, LANES), jnp.float32)


def solve_chain(chain):
    size, middle = len(chain), len(chain) // 2
    slope, value = [None] * size, [None] * size
    for k in range(middle):
        for m, before in ((k, k - 1), (size - 1 - k, size - k)):
            low, diag, up, rhs = chain[m]
            outer, inner = (low, up) if m < middle else (up, low)
            if k > 0:
                diag = diag - outer * slope[before]
                rhs = rhs - outer * value[before]
            inverse = 1.0 / diag
            value[m] = rhs * inverse
            slope[m] = inner * inverse
    a, b = middle - 1, middle
    value[a] = (value[a] - slope[a] * value[b]) * (1.0 / (1.0 - slope[a] * slope[b]))
    value[b] = value[b] - slope[b] * value[a]
    for k in range(middle - 2, -1, -1):
        value[k] = value[k] - slope[k] * value[k + 1]
        m = size - 1 - k
        value[m] = value[m] - slope[m] * value[m - 1]
    return value


def join(blocks, at_ends):
    count = len(blocks)
    one = lambda b, row: blocks[b](row, 1)
    face = lambda b: 0.5 * (one(b, 15) + one(b + 1, 7))
    chain, deltas, scales = [], [], []
    for b in range(count):
        rhs_first, rhs_last = blocks[b](0, 8), blocks[b](8, 8)
        second = before = None
        if b > 0:
            second = blocks[b - 1](ROW_FLUX_RIGHT, 8)
            rhs_first = rhs_first + blocks[b - 1](ROW_RIGHT, 8) + one(b, 5) * second
            rhs_last = rhs_last + one(b, 6) * second
        if b < count - 1:
            before = blocks[b + 1](ROW_FLUX_LEFT, 8)
            rhs_first = rhs_first + one(b, 13) * before
            rhs_last = rhs_last + blocks[b + 1](ROW_LEFT, 8) + one(b, 14) * before
        up, low = ONE_THIRD - one(b, ROW_HI), ONE_THIRD - one(b, ROW_LO)
        lo_first = face(b - 1) if b > 0 else 0.5 * one(b, 7)
        hi_last = face(b) if b < count - 1 else 0.5 * one(b, 15)
        zero = jnp.zeros_like(up)
        outer_low = ONE_THIRD - lo_first if b > 0 else zero
        outer_up = ONE_THIRD - hi_last if b < count - 1 else zero
        chain.append((outer_low, (1.0 + lo_first + one(b, ROW_HI)) + up * one(b, 5), up * one(b, 6), rhs_first))
        chain.append((low * one(b, 13), (1.0 + one(b, ROW_LO) + hi_last) + low * one(b, 14), outer_up, rhs_last))
        deltas.append((second, before))
        scales.append((up, low))
    return chain if at_ends else chain[1:-1], chain[0], chain[-1], deltas, scales


def ordered(stage, place, pay_refs, blocks_ref):
    for k, pay_ref in zip((0,) + tuple(stage[2]), pay_refs):
        blocks_ref[jnp.bitwise_xor(place, k)] = pay_ref[...]
    return [lambda row, size, b=b: blocks_ref[b, :, row : row + size, :] for b in range(len(pay_refs))]


def place_in(stage, me_ref):
    first, size, _ = stage
    return lax.rem(me_ref[0] // first, size)


def merge_kernel(stage, me_ref, *refs):
    size = stage[1]
    pay_refs, (merged_ref, own_ref, blocks_ref, table_ref) = refs[:size], refs[size:]
    place = place_in(stage, me_ref)
    blocks = ordered(stage, place, pay_refs, blocks_ref)
    chain, first, last, deltas, scales = join(blocks, False)
    eight = sublane_ids((2, 8, LANES))
    is_field = eight < FIELDS
    rhs = [jnp.where(is_field, value, 0.0) for _, _, _, value in chain]
    rhs[0] = jnp.where(eight == 5, -chain[0][0], rhs[0])
    rhs[-1] = jnp.where(eight == 6, -chain[-1][2], rhs[-1])
    inner = solve_chain([(low, diag, up, value) for (low, diag, up, _), value in zip(chain, rhs)])

    merged_ref[:, 0:8, :] = first[3] - first[2] * inner[0]
    merged_ref[:, 8:16, :] = last[3] - last[0] * inner[-1]
    merged_ref[:, 5:6, :] = blocks[0](5, 1) + blocks[0](6, 1) * inner[0][:, 5:6, :]
    merged_ref[:, 6:7, :] = blocks[0](6, 1) * inner[0][:, 6:7, :]
    merged_ref[:, 7:8, :] = blocks[0](7, 1)
    merged_ref[:, 13:14, :] = blocks[-1](13, 1) * inner[-1][:, 5:6, :]
    merged_ref[:, 14:15, :] = blocks[-1](14, 1) + blocks[-1](13, 1) * inner[-1][:, 6:7, :]
    merged_ref[:, 15:16, :] = blocks[-1](15, 1)
    for row, rows, block in (
        (ROW_RIGHT, 5, -1), (ROW_HI, 1, 0), (ROW_FLUX_RIGHT, 5, -1), (ROW_LEFT, 10, 0), (ROW_LO, 1, -1)
    ):
        merged_ref[:, row : row + rows, :] = blocks[block](row, rows)
    merged_ref[:, 38:40, :] = jnp.zeros((2, 2, LANES), jnp.float32)

    for b in range(size):
        zero = jnp.zeros((2, 8, LANES), jnp.float32)
        own_first = jnp.where((eight == 5) | (eight == 7), 1.0, zero) if b == 0 else inner[2 * b - 1]
        own_last = jnp.where((eight == 6) | (eight == 7), 1.0, zero) if b == size - 1 else inner[2 * b]
        second, before = deltas[b]
        second = zero if second is None else jnp.where(is_field, second / scales[b][0], 0.0)
        before = zero if before is None else jnp.where(is_field, before / scales[b][1], 0.0)
        for i, value in enumerate((own_first, own_last, second, before)):
            table_ref[:, b * 32 + 8 * i : b * 32 + 8 * i + 8, :] = value
    own_ref[...] = table_ref[:, pl.ds(pl.multiple_of(place * 32, 32), 32), :]


def outer_solve(stage, me_ref, pay_refs, own_refs, blocks_ref, table_ref):
    place = place_in(stage, me_ref)
    chain, _, _, deltas, scales = join(ordered(stage, place, pay_refs, blocks_ref), True)
    solved = solve_chain(chain)
    for b in range(stage[1]):
        x_first, x_last = solved[2 * b], solved[2 * b + 1]
        second, before = deltas[b]
        seen_first = x_first if second is None else x_first - second / scales[b][0]
        seen_last = x_last if before is None else x_last - before / scales[b][1]
        for i, value in enumerate((x_first, x_last, seen_first, seen_last)):
            table_ref[:, b * 32 + 8 * i : b * 32 + 8 * i + 8, :] = value
    mine = table_ref[:, pl.ds(pl.multiple_of(place * 32, 32), 32), :]
    ends = [mine[:, 8 * i : 8 * i + 8] for i in range(4)]
    for own_ref in own_refs:
        x_first, x_last, seen_first, seen_last = ends
        own_first, own_last, second, before = (own_ref[:, 8 * i : 8 * i + 8, :] for i in range(4))
        first = own_first + own_first[:, 5:6] * seen_first + own_first[:, 6:7] * seen_last
        last = own_last + own_last[:, 5:6] * seen_first + own_last[:, 6:7] * seen_last
        ends = [
            first + own_first[:, 7:8] * (x_first - seen_first),
            last + own_last[:, 7:8] * (x_last - seen_last),
            first - second,
            last - before,
        ]
    return [[value[h] for value in ends] for h in range(2)]


def rebuild(ends, count, part_ref, left_ref, right_ref, inner_ref, sol_ref):
    x_first, x_last, seen_first, seen_last = ends
    for m in range(16):
        if m == 0:
            value = seen_first
        elif m == 15:
            value = seen_last
        else:
            inner = inner_ref[8 * m : 8 * m + 8, :]
            value = inner + inner[5:6] * seen_first + inner[6:7] * seen_last
        sol_ref[8 * m : 8 * m + 8, :] = value
    chunk_first = [sol_ref[pl.ds(q, CHUNKS, stride=16), :] for q in range(FIELDS)]
    chunk_last = [sol_ref[pl.ds(8 + q, CHUNKS, stride=16), :] for q in range(FIELDS)]
    ids = sublane_ids(chunk_first[0].shape)

    def solution_at(q, j):
        if j == 0:
            return jnp.where(ids == 0, x_first[q : q + 1], chunk_first[q])
        if j == count - 1:
            return jnp.where(ids == CHUNKS - 1, x_last[q : q + 1], chunk_last[q])
        here = pl.ds(j * CHUNKS, CHUNKS)
        return part_ref[q, here, :] + left_ref[here, :] * chunk_first[q] + right_ref[here, :] * chunk_last[q]

    return solution_at


def turn(count, from_ref, to_ref):
    for k in range(2):
        starts = [64 * t + c for c in range(4 * k, 4 * k + 4) for t in range(count // 8)]
        for i in range(2):
            tiles = [from_ref[i, pl.ds(start, 8, stride=CHUNKS), :] for start in starts]
            to_ref[k, i * LANES : (i + 1) * LANES, :] = jnp.concatenate(tiles, 0).T


def lane_half(h):
    return pl.ds(h * LANES, LANES)


def x_kernel(
    count, state_ref, viscous_ref, part_ref, left_ref, right_ref, inner_ref, pay_ref, aux_ref,
    held_ref, first_ref, last_ref, sems,
):
    copies = [
        pltpu.make_async_copy(viscous_ref.at[:, lane_half(h)], held_ref.at[h, FIELDS], sems.at[h, FIELDS])
        for h in range(2)
    ] + [
        pltpu.make_async_copy(state_ref.at[q, :, lane_half(h)], held_ref.at[h, q], sems.at[h, q])
        for h in range(2)
        for q in range(FIELDS)
    ]
    for copy in copies:
        copy.start()
    for copy in copies[:2]:
        copy.wait()

    def ready(h):
        for copy in copies[2 + FIELDS * h : 2 + FIELDS * (h + 1)]:
            copy.wait()

    def make_terms(h, j):
        density, mom_x, mom_y, mom_z, energy = (strided(held_ref.at[h, q], j, count) for q in range(FIELDS))
        inverse = 1.0 / density
        vel_x = (NEAR_SCALED * inverse) * mom_x
        kinetic = mom_x * mom_x + mom_y * mom_y + mom_z * mom_z
        press = GAMMA_MINUS * (energy - 0.5 * kinetic * inverse)
        here = pl.ds(j * CHUNKS, CHUNKS)
        aux_ref[h, 0, here, :] = (NEAR_SCALED * inverse) * mom_y
        aux_ref[h, 1, here, :] = press
        low, high, far = ONE_THIRD - vel_x, ONE_THIRD + vel_x, FAR_RATIO * vel_x

        def general(u, flux):
            third = ONE_THIRD * u
            return u, third - flux, third + flux, FAR_RATIO * flux

        def carried(u):
            return u, low * u, high * u, far * u

        return (
            general(density, NEAR_SCALED * mom_x),
            general(mom_x, mom_x * vel_x + NEAR_SCALED * press),
            carried(mom_y),
            carried(mom_z),
            general(energy, (energy + press) * vel_x),
        )

    def viscous_at(j):
        value = jnp.stack([strided(held_ref.at[h, FIELDS], j, count) for h in range(2)])
        aux_ref[:, 2, pl.ds(j * CHUNKS, CHUNKS), :] = value
        return value

    matrix, factors = Matrix(viscous_at, count), ({}, {}, {}, Rows(left_ref), Rows(right_ref))
    eliminate_matrix(matrix, *factors)
    local_solve(ready, make_terms, matrix, factors, part_ref, inner_ref, pay_ref, first_ref, last_ref)


def y_matrix_kernel(count, aux_ref, turned_ref, inverse_ref, tied_ref, slope_ref, left_ref, right_ref):
    for i in range(3):
        turn(count, aux_ref.at[:, i], turned_ref.at[i])
    matrix = Matrix(lambda j: jnp.stack([strided(turned_ref.at[2, h], j, count) for h in range(2)]), count)
    eliminate_matrix(matrix, *map(Rows, (inverse_ref, tied_ref, slope_ref, left_ref, right_ref)))
    inverse_ref[:, (count - 1) * CHUNKS :, :] = jnp.zeros((2, CHUNKS, LANES), jnp.float32)


def y_kernel(count, stages, me_ref, *refs):
    size, levels = stages[-1][1], len(stages) - 1
    pay_refs, own_refs, refs = refs[:size], refs[size : size + levels], refs[size + levels :]
    x_part_ref, x_left_ref, x_right_ref, x_inner_ref, aux_ref, *refs = refs
    inverse_ref, tied_ref, slope_ref, left_ref, right_ref, part_ref, inner_ref, pay_ref, *refs = refs
    blocks_ref, table_ref, sol_ref, section_ref, turned_ref, first_ref, last_ref = refs
    ends = outer_solve(stages[-1], me_ref, pay_refs, own_refs, blocks_ref, table_ref)
    halves = [
        rebuild(
            ends[h], count, x_part_ref.at[h], x_left_ref.at[h], x_right_ref.at[h], x_inner_ref.at[h], sol_ref.at[h]
        )
        for h in range(2)
    ]
    for q in range(FIELDS):
        for h in range(2):
            for j in range(count):
                section_ref[q, h, pl.ds(j * CHUNKS, CHUNKS), :] = halves[h](q, j)
        turn(count, section_ref.at[q], turned_ref.at[q])

    def value(q, h, j):
        return strided(turned_ref.at[q, h], j, count)

    def make_terms(h, j):
        vel_y, press = strided(aux_ref.at[0, h], j, count), strided(aux_ref.at[1, h], j, count)
        low, high, far = ONE_THIRD - vel_y, ONE_THIRD + vel_y, FAR_RATIO * vel_y

        def carried(u):
            return u, low * u, high * u, far * u

        def pressed(u, flux):
            return u, low * u - flux, high * u + flux, far * u + FAR_RATIO * flux

        return (
            carried(value(0, h, j)),
            carried(value(1, h, j)),
            pressed(value(2, h, j), NEAR_SCALED * press),
            carried(value(3, h, j)),
            pressed(value(4, h, j), press * vel_y),
        )

    def viscous_at(j):
        return jnp.stack([strided(aux_ref.at[2, h], j, count) for h in range(2)])

    factors = tuple(map(Rows, (inverse_ref, tied_ref, slope_ref, left_ref, right_ref)))
    local_solve(
        lambda h: None, make_terms, Matrix(viscous_at, count), factors,
        part_ref, inner_ref, pay_ref, first_ref, last_ref,
    )


def last_kernel(count, stages, me_ref, *refs):
    size, levels = stages[-1][1], len(stages) - 1
    pay_refs, own_refs, refs = refs[:size], refs[size : size + levels], refs[size + levels :]
    part_ref, left_ref, right_ref, inner_ref, new_ref, *refs = refs
    blocks_ref, table_ref, sol_ref, section_ref, turned_ref, sems = refs
    ends = outer_solve(stages[-1], me_ref, pay_refs, own_refs, blocks_ref, table_ref)
    halves = [
        rebuild(ends[h], count, part_ref.at[h], left_ref.at[h], right_ref.at[h], inner_ref.at[h], sol_ref.at[h])
        for h in range(2)
    ]
    copies = []
    for q in range(FIELDS):
        for h in range(2):
            for j in range(count):
                section_ref[q, h, pl.ds(j * CHUNKS, CHUNKS), :] = halves[h](q, j)
        turn(count, section_ref.at[q], turned_ref.at[q])
        for h in range(2):
            copies.append(
                pltpu.make_async_copy(turned_ref.at[q, h], new_ref.at[q, :, lane_half(h)], sems.at[q, h])
            )
            copies[-1].start()
    for copy in copies:
        copy.wait()


def shards(devices_x, devices_y, state, viscous):
    cells = state.shape[2]
    count = cells // CHUNKS
    float_of = lambda *shape: jax.ShapeDtypeStruct(shape, jnp.float32)
    memory = lambda *shape: pltpu.VMEM(shape, jnp.float32)
    params = pltpu.CompilerParams(vmem_limit_bytes=48 * 1024 * 1024)
    whole = pl.BlockSpec(memory_space=pltpu.VMEM)
    far = pl.BlockSpec(memory_space=pltpu.HBM)
    scalar = pl.BlockSpec(memory_space=pltpu.SMEM)
    solved_shapes = [
        float_of(2, FIELDS, cells, LANES), float_of(2, cells, LANES), float_of(2, cells, LANES),
        float_of(2, 128, LANES),
    ]
    pay_shape = (2, PAY_ROWS, LANES)
    *x_parts, x_pay, aux = pl.pallas_call(
        functools.partial(x_kernel, count),
        out_shape=solved_shapes + [float_of(*pay_shape), float_of(2, 3, cells, LANES)],
        in_specs=[far] * 2,
        out_specs=[whole] * 6,
        scratch_shapes=[
            memory(2, FIELDS + 1, cells, LANES), memory(2, 72, LANES), memory(2, 72, LANES),
            pltpu.SemaphoreType.DMA((2, FIELDS + 1)),
        ],
        compiler_params=params,
        name="x_lines",
    )(
        pltpu.with_memory_space_constraint(state.reshape(FIELDS, cells, cells), pltpu.HBM),
        pltpu.with_memory_space_constraint(viscous.reshape(cells, cells), pltpu.HBM),
    )
    me = (lax.axis_index("gx") * devices_y + lax.axis_index("gy")).astype(jnp.int32).reshape(1)
    def merge_scratch(stage):
        return [memory(stage[1], *pay_shape), memory(2, 32 * stage[1], LANES)]

    def gather(pay, axis, stages):
        owns = []
        for stage in stages:
            pays = [pay]
            for mask in stage[2].values():
                pairs = [(i, i ^ mask) for i in range(lax.axis_size(axis))]
                pays.append(lax.ppermute(pay, axis, pairs))
            if stage is stages[-1]:
                return pays + owns[::-1]
            pay, own = pl.pallas_call(
                functools.partial(merge_kernel, stage),
                out_shape=[float_of(*pay_shape), float_of(2, 32, LANES)],
                in_specs=[scalar] + [whole] * stage[1],
                out_specs=[whole] * 2,
                scratch_shapes=merge_scratch(stage),
                compiler_params=params,
                name="merge_" + axis,
            )(me, *pays)
            owns.append(own)

    x_stages = (
        (devices_y, 2, {1: 1}),
        (2 * devices_y, 4, {1: 2, 2: 4, 3: 6}),
        (8 * devices_y, 2, {1: 12}),
    )
    y_stages = ((1, 4, {1: 1, 3: 3, 2: 2}), (4, 4, {1: 4, 3: 12, 2: 8}))
    x_ends = gather(x_pay, "gx", x_stages)
    plane = float_of(2, cells, LANES)
    y_aux, *y_factors = pl.pallas_call(
        functools.partial(y_matrix_kernel, count),
        out_shape=[float_of(3, 2, cells, LANES)] + [plane] * 5,
        in_specs=[whole],
        out_specs=[whole] * 6,
        compiler_params=params,
        cost_estimate=pl.CostEstimate(flops=4000000, bytes_accessed=2000000, transcendentals=0),
        name="y_matrix",
    )(aux)
    y_part, y_inner, y_pay = pl.pallas_call(
        functools.partial(y_kernel, count, x_stages),
        out_shape=[solved_shapes[0], solved_shapes[3], float_of(*pay_shape)],
        in_specs=[scalar] + [whole] * (len(x_ends) + 10),
        out_specs=[whole] * 3,
        scratch_shapes=merge_scratch(x_stages[-1]) + [
            memory(2, 128, LANES), memory(FIELDS, 2, cells, LANES), memory(FIELDS, 2, cells, LANES),
            memory(2, 72, LANES), memory(2, 72, LANES),
        ],
        compiler_params=params,
        name="y_lines",
    )(me, *x_ends, *x_parts, y_aux, *y_factors)
    y_ends = gather(y_pay, "gy", y_stages)
    new = pl.pallas_call(
        functools.partial(last_kernel, count, y_stages),
        out_shape=float_of(FIELDS, cells, cells),
        in_specs=[scalar] + [whole] * (len(y_ends) + 4),
        out_specs=far,
        scratch_shapes=merge_scratch(y_stages[-1]) + [
            memory(2, 128, LANES), memory(FIELDS, 2, cells, LANES), memory(FIELDS, 2, cells, LANES),
            pltpu.SemaphoreType.DMA((FIELDS, 2)),
        ],
        compiler_params=params,
        name="new_state",
    )(me, *y_ends, y_part, *y_factors[3:], y_inner)
    return new.reshape(state.shape)


def solution(mesh):
    placed = (P(None, None, "gx", "gy"), P(None, "gx", "gy"))
    return jax.shard_map(
        functools.partial(shards, mesh.shape["gx"], mesh.shape["gy"]),
        mesh=mesh, in_specs=placed, out_specs=P(None, None, "gx", "gy"), check_vma=False,
    )
```
